768 devices in a mesh: wire: 128 (over z_hi, y, x, core), depth: 6 (over z_lo).
Axes of the slice: x: 4, y: 8, z: 12 (z_hi: 2, z_lo: 6; z = z_hi * 6 + z_lo), core: 2. Of those that a mesh axis runs over, the one named last changes fastest.
Arguments:
- density: float32 [768, 64, 1600], P('wire'), as said below
- pattern: int32 [768, 25], P('wire'), may hold values from 0 to 1, as said below
Outputs:
- purified: float32 [768, 64, 1600], P(('wire', 'depth'))
The draws below stay inside these ranges and needn't reach their ends.
Inputs may be any that keep to these rules, and one draw needn't show every extreme that they name: The pattern is symmetric: pattern[i, d] equals pattern[(i + d - 12) mod 768, 24 - d]; the diagonal block is always present. The density matrix is symmetric and its blocks are zero where the pattern is 0.
All inputs are finite; a program needn't handle non-finite values.
Results may differ from the reference program's by a relative error of at most 0.0001.
Values sent between devices are 32-bit elements; how exact they have to be, the bound alone decides.
A program may use at most 64 MiB of HBM per device.

```python
import jax
import jax.numpy as jnp
from jax import lax

ORB = 64
HALF = 12
NB = 768


def pattern_bits(key):
    sub = jax.random.fold_in(key, 11)
    upper = (jax.random.randint(sub, (NB, HALF), 0, 4) > 0).astype(jnp.int32)
    columns = []
    for offset in range(2 * HALF + 1):
        if offset < HALF:
            columns.append(jnp.roll(upper[:, HALF - 1 - offset], HALF - offset, axis=0))
        elif offset == HALF:
            columns.append(jnp.ones((NB,), jnp.int32))
        else:
            columns.append(upper[:, offset - HALF - 1])
    return jnp.stack(columns, axis=1)


def draw_pattern(key, part):
    return pattern_bits(key)


def draw_density(key, part):
    mask = pattern_bits(key).astype(jnp.float32)
    upper_key = jax.random.fold_in(key, 23)
    diag_key = jax.random.fold_in(key, 29)
    filled_key = jax.random.fold_in(key, 31)
    scale = 0.01
    filled = jax.random.randint(filled_key, (NB, ORB), 0, 2).astype(jnp.float32)
    upper = jax.random.normal(upper_key, (NB, HALF, ORB, ORB), jnp.float32) * scale
    middle = jax.random.normal(diag_key, (NB, ORB, ORB), jnp.float32) * scale
    high_level = 0.95
    low_level = 0.05
    occupation = low_level + (high_level - low_level) * filled
    middle = 0.5 * (middle + jnp.swapaxes(middle, 1, 2)) + occupation[:, :, None] * jnp.eye(ORB, dtype=jnp.float32)[None]
    blocks = []
    for offset in range(2 * HALF + 1):
        if offset < HALF:
            mirror = jnp.roll(upper[:, HALF - 1 - offset], HALF - offset, axis=0)
            blocks.append(jnp.swapaxes(mirror, 1, 2))
        elif offset == HALF:
            blocks.append(middle)
        else:
            blocks.append(upper[:, offset - HALF - 1])
    stacked = jnp.stack(blocks, axis=1) * mask[:, :, None, None]
    return jnp.transpose(stacked, (0, 2, 1, 3)).reshape(NB, ORB, (2 * HALF + 1) * ORB)


def setup_inputs(seed: int = 0) -> dict:
    key_list = jax.random.split(jax.random.key(seed), 3)
    return {
        "density": draw_density(jax.random.fold_in(key_list[2], 71), 0),
        "pattern": draw_pattern(jax.random.fold_in(key_list[2], 71), 0),
    }


def band_product(left, right):
    count, orb, cols = left.shape
    width = cols // orb
    half = (width - 1) // 2
    total = jnp.zeros((count, orb, cols), jnp.float32)
    for offset in range(width):
        block = left[:, :, offset * orb:(offset + 1) * orb]
        rolled = jnp.roll(right, -(offset - half), axis=0)
        term = jnp.einsum('nab,nbc->nac', block, rolled, precision=lax.Precision.HIGHEST)
        padded = jnp.pad(term, ((0, 0), (0, 0), (half * orb, half * orb)))
        start = (2 * half - offset) * orb
        total = total + padded[:, :, start:start + cols]
    return total


def reference(density, pattern):
    orb = density.shape[1]
    maskband = jnp.repeat(pattern.astype(jnp.float32), orb, axis=1)[:, None, :]
    square = band_product(density, density) * maskband
    cube = band_product(square, density) * maskband
    return 3.0 * square - 2.0 * cube
```

```python
import jax
import jax.numpy as jnp
from jax import lax
from jax.experimental import pallas as pl
from jax.experimental.pallas import tpu as pltpu
from jax.sharding import PartitionSpec as P

MESH = pl.DeviceIdType.MESH
ORB = 64
ROWS = 6
CHIP = 2 * ROWS
FRAME = 3 * CHIP * ORB
SIDE = CHIP * ORB
HALFSIDE = ROWS * ORB
BAND = 25 * ORB
BANDPAD = 26 * ORB
TILE = 256
DIAG = 12 * ORB
F32 = jnp.float32
BF16 = jnp.bfloat16


def member():
    return lax.axis_index("depth")


def lanes(blocks):
    return (blocks + 1) // 2 * 2 * ORB


def split(x):
    high = x.astype(BF16)
    low = (x - high.astype(F32)).astype(BF16)
    return high, low


def symmetrized(tile):
    size = tile.shape[0]
    row = lax.broadcasted_iota(jnp.int32, (size, size), 0) >> 6
    col = lax.broadcasted_iota(jnp.int32, (size, size), 1) >> 6
    tile = tile.astype(F32)
    return jnp.where(row <= col, tile, tile.T).astype(BF16)


def kernel(
    density, pattern, out,
    rows, big, small, wc_hi, wc_lo, big_hi, big_lo, small_hi, small_lo,
    left, middle, square, cube, maskrow,
    own_sem, pair_send, pair_recv, up_send, down_send, big_recv, fwd_send, fwd_recv,
):
    wire = lax.axis_index("wire")
    length = lax.axis_size("wire")
    m = member()
    h = lax.rem(wire, 2)
    other = wire + 1 - 2 * h
    up = lax.rem(wire - h + 2, length)
    down = lax.rem(wire - h - 1 + length, length)
    source = lax.rem(wire - h + 4 * h - 2 + length, length)

    own = pltpu.make_async_copy(density, rows.at[pl.ds(ROWS * h, ROWS)], own_sem)
    own.start()

    barrier = pltpu.get_barrier_semaphore()
    for sender in (other, source, source + 1):
        pl.semaphore_signal(barrier, inc=1, device_id={"wire": sender}, device_id_type=MESH)
    pl.semaphore_wait(barrier, 3)

    pair = pltpu.make_async_remote_copy(
        src_ref=density, dst_ref=rows.at[pl.ds(ROWS * h, ROWS)],
        send_sem=pair_send, recv_sem=pair_recv,
        device_id={"wire": other}, device_id_type=MESH,
    )

    def outgoing(core):
        copies = []
        for s in range(ROWS):
            t = ROWS * core + s
            width = lanes(CHIP - t)
            for target, sem in ((up, up_send), (down, down_send)):
                copies.append(pltpu.make_async_remote_copy(
                    src_ref=density.at[s, :, pl.ds(DIAG, width)],
                    dst_ref=big.at[t, :, pl.ds(0, width)],
                    send_sem=sem.at[s], recv_sem=big_recv.at[t],
                    device_id={"wire": target}, device_id_type=MESH,
                ))
        return copies

    def arriving(t):
        width = lanes(CHIP - t)
        return pltpu.make_async_remote_copy(
            src_ref=density.at[t % ROWS, :, pl.ds(DIAG, width)],
            dst_ref=big.at[t, :, pl.ds(0, width)],
            send_sem=up_send.at[t % ROWS], recv_sem=big_recv.at[t],
            device_id={"wire": up}, device_id_type=MESH,
        )

    def forward(s):
        width = lanes(ROWS - s)
        return pltpu.make_async_remote_copy(
            src_ref=big.at[ROWS * (1 - h) + s, :, pl.ds(0, width)],
            dst_ref=small.at[s, :, pl.ds(0, width)],
            send_sem=fwd_send.at[s], recv_sem=fwd_recv.at[s],
            device_id={"wire": other}, device_id_type=MESH,
        )

    for core in range(2):
        @pl.when(h == core)
        def _(core=core):
            for copy in outgoing(core):
                copy.start()
    pair.start()

    wc_hi[...] = jnp.zeros_like(wc_hi)
    wc_lo[...] = jnp.zeros_like(wc_lo)
    place = ROWS * h + m

    def band_row(index):
        x = rows[index]
        return jnp.concatenate([x, jnp.zeros((ORB, BANDPAD - BAND), F32)], axis=1)

    def build_centre(half):
        for s in range(ROWS):
            x = band_row(ROWS * half + s)
            if s % 2:
                x = pltpu.roll(x, ORB, 1)
            high, low = split(x)
            down_by = pl.ds(pl.multiple_of(half * HALFSIDE + s * ORB, ORB), ORB)
            along = pl.ds(pl.multiple_of(half * HALFSIDE + (s - s % 2) * ORB, 128), BANDPAD)
            wc_hi[down_by, along] = high
            wc_lo[down_by, along] = low

    own.wait()
    build_centre(h)

    def framed(x):
        wide = jnp.concatenate([x, jnp.zeros((x.shape[0], FRAME - BANDPAD), F32)], axis=1)
        return pltpu.roll(wide, place * ORB, 1)

    def stack(ref, x, along):
        high, low = split(x)
        ref[0:ORB, along] = high
        ref[ORB:2 * ORB, along] = low

    stack(left, framed(band_row(place)), slice(0, FRAME))

    block = lax.broadcasted_iota(jnp.int32, (8, BANDPAD), 1) >> 6
    bits = jnp.zeros((8, BANDPAD), F32)
    for d in range(25):
        bits = jnp.where(block == d, pattern[m, d].astype(F32), bits)
    maskrow[...] = framed(bits)

    def product(ref, along, high, low, across):
        dims = (((1,), (1 if across else 0,)), ((), ()))
        first = lax.dot_general(ref[:, along], high, dims, preferred_element_type=F32)
        second = lax.dot_general(ref[0:ORB, along], low, dims, preferred_element_type=F32)
        return first[0:ORB] + first[ORB:2 * ORB] + second

    def centre(ref, acc):
        for b in range(9):
            a0, a1 = max(0, b - 6), min(3, b + 1)
            down_by = slice(a0 * TILE, a1 * TILE)
            along = slice(b * TILE, (b + 1) * TILE)
            acc[:, along] = product(
                ref, slice(SIDE + a0 * TILE, SIDE + a1 * TILE),
                wc_hi[down_by, along], wc_lo[down_by, along], False,
            )

    def sides(ref, acc):
        for a in range(3):
            down_by = slice(a * TILE, (a + 1) * TILE)
            lo = slice(a * TILE, SIDE)
            hi = slice(2 * SIDE, 2 * SIDE + (a + 1) * TILE)
            acc[:, SIDE + a * TILE:SIDE + (a + 1) * TILE] += (
                product(ref, lo, wc_hi[down_by, lo], wc_lo[down_by, lo], True)
                + product(ref, hi, wc_hi[down_by, hi], wc_lo[down_by, hi], True)
            )

    big_at = h * (2 * SIDE)
    small_at = 2 * SIDE - h * (2 * SIDE - HALFSIDE)

    def corners(ref, acc):
        for b in range(3):
            here = pl.ds(pl.multiple_of(big_at + b * TILE, 128), TILE)
            upto = (b + 1) * TILE
            total = product(
                ref, pl.ds(pl.multiple_of(big_at, 128), upto),
                big_hi[0:upto, b * TILE:upto], big_lo[0:upto, b * TILE:upto], False,
            )
            if b < 2:
                total += product(
                    ref, pl.ds(pl.multiple_of(big_at + upto, 128), SIDE - upto),
                    big_hi[b * TILE:upto, upto:SIDE], big_lo[b * TILE:upto, upto:SIDE], True,
                )
            acc[:, here] += total
        here = pl.ds(pl.multiple_of(small_at, 128), HALFSIDE)
        acc[:, here] += product(ref, here, small_hi[...], small_lo[...], False)

    pair.wait_recv()
    build_centre(1 - h)

    centre(left, square)
    sides(left, square)
    mid = slice(SIDE, 2 * SIDE)
    masked = square[:, mid] * maskrow[0:1, mid]
    square[:, mid] = masked
    stack(middle, masked, mid)
    centre(middle, cube)

    for core in range(2):
        @pl.when(h == core)
        def _(core=core):
            for s in range(ROWS):
                arriving(ROWS * (1 - core) + s).wait_recv()
    for s in range(ROWS):
        forward(s).start()
    for core in range(2):
        @pl.when(h == core)
        def _(core=core):
            for s in range(ROWS):
                arriving(ROWS * core + s).wait_recv()

    def build_triangle(source_ref, high_ref, low_ref, count):
        for t in range(count):
            x = source_ref[t, :, 0:lanes(count - t)]
            if t % 2:
                x = pltpu.roll(x, ORB, 1)
                lane = lax.broadcasted_iota(jnp.int32, x.shape, 1)
                x = jnp.where(lane < ORB, 0.0, x)
            high, low = split(x)
            along = slice((t - t % 2) * ORB, count * ORB)
            high_ref[t * ORB:(t + 1) * ORB, along] = high
            low_ref[t * ORB:(t + 1) * ORB, along] = low

    build_triangle(big, big_hi, big_lo, CHIP)
    for ref in (big_hi, big_lo):
        for a in range(3):
            tile = slice(a * TILE, (a + 1) * TILE)
            ref[tile, tile] = symmetrized(ref[tile, tile])
    for s in range(ROWS):
        forward(s).wait_recv()
    build_triangle(small, small_hi, small_lo, ROWS)
    for ref in (small_hi, small_lo):
        ref[...] = symmetrized(ref[...])

    corners(left, square)
    for along in (slice(0, SIDE), slice(2 * SIDE, FRAME)):
        masked = square[:, along] * maskrow[0:1, along]
        square[:, along] = masked
        stack(middle, masked, along)
    sides(middle, cube)
    corners(middle, cube)

    result = 3.0 * square[...] - 2.0 * (cube[...] * maskrow[0:1, :])
    out[0] = pltpu.roll(result, FRAME - place * ORB, 1)[:, 0:BAND]

    for core in range(2):
        @pl.when(h == core)
        def _(core=core):
            for copy in outgoing(core):
                copy.wait_send()
    pair.wait_send()
    for s in range(ROWS):
        forward(s).wait_send()


def on_device(density, pattern):
    dma = pltpu.SemaphoreType.DMA
    return pl.pallas_call(
        kernel,
        out_shape=jax.ShapeDtypeStruct((1, ORB, BAND), F32),
        in_specs=[pl.BlockSpec(memory_space=pl.ANY), pl.BlockSpec(memory_space=pltpu.SMEM)],
        out_specs=pl.BlockSpec(memory_space=pltpu.VMEM),
        scratch_shapes=[
            pltpu.VMEM((CHIP, ORB, BAND), F32),
            pltpu.VMEM((CHIP, ORB, SIDE), F32),
            pltpu.VMEM((ROWS, ORB, HALFSIDE), F32),
            pltpu.VMEM((SIDE, FRAME), BF16),
            pltpu.VMEM((SIDE, FRAME), BF16),
            pltpu.VMEM((SIDE, SIDE), BF16),
            pltpu.VMEM((SIDE, SIDE), BF16),
            pltpu.VMEM((HALFSIDE, HALFSIDE), BF16),
            pltpu.VMEM((HALFSIDE, HALFSIDE), BF16),
            pltpu.VMEM((2 * ORB, FRAME), BF16),
            pltpu.VMEM((2 * ORB, FRAME), BF16),
            pltpu.VMEM((ORB, FRAME), F32),
            pltpu.VMEM((ORB, FRAME), F32),
            pltpu.VMEM((8, FRAME), F32),
            dma, dma, dma, dma((ROWS,)), dma((ROWS,)), dma((CHIP,)), dma((ROWS,)), dma((ROWS,)),
        ],
        compiler_params=pltpu.CompilerParams(
            collective_id=0, has_side_effects=True, vmem_limit_bytes=48 * 1024 * 1024
        ),
    )(density, pattern)


def solution(mesh):
    in_specs = (P("wire", None, None), P("wire", None))
    out_specs = P(("wire", "depth"), None, None)
    return jax.shard_map(
        on_device, mesh=mesh, in_specs=in_specs, out_specs=out_specs, check_vma=False
    )
```

```python
import jax
import jax.numpy as jnp
from jax import lax
from jax.experimental import pallas as pl
from jax.experimental.pallas import tpu as pltpu
from jax.sharding import PartitionSpec as P

MESH = pl.DeviceIdType.MESH
ORB = 64
ROWS = 6
CHIP = 2 * ROWS
FRAME = 3 * CHIP * ORB
SIDE = CHIP * ORB
HALFSIDE = ROWS * ORB
BAND = 25 * ORB
BANDPAD = 26 * ORB
TILE = 256
DIAG = 12 * ORB
F32 = jnp.float32
BF16 = jnp.bfloat16


FIRST = (8, 10, 5, 2, 1, 0)
SECOND = (6, 7, 9, 11, 4, 3)
LEFT_ORDER = (
    (8, 10, 5, 2, 1, 6, 7, 9, 11, 4, 3, 0),
    (8, 10, 5, 6, 7, 9, 11, 2, 4, 1, 3),
    (6, 7, 9, 11, 8, 10, 5, 4, 3, 2),
    (6, 7, 9, 11, 4, 3, 8, 10, 5),
    (6, 7, 9, 11, 4, 8, 10, 5),
    (6, 7, 9, 11, 8, 10, 5),
)
LEFT_NEXT = (
    {1: FIRST},
    {2: FIRST, 0: SECOND},
    {3: FIRST + SECOND, 1: SECOND},
    {4: FIRST + SECOND},
    {5: FIRST + SECOND},
    {},
)
RIGHT_REACH = (9, 9, 9, 10, 11, 12)
RIGHT_NEXT = ((1,), (2,), (), (), (3,), (4,))
NEXT = (LEFT_NEXT, RIGHT_NEXT)
ENTRY = ({5: 0, 0: 2}, {5: 0, 0: 5})
EARLY_GIVER = (((1, 0), (1, 2), (2, 3), (3, 4), (4, 5)), ((0, 1), (1, 2)))
NEAR_FIRST = (6, 0, 7, 8, 1, 9, 10, 11, 2, 3, 4, 5)


def lanes(blocks):
    return (blocks + 1) // 2 * 2 * ORB


def split(x):
    high = x.astype(BF16)
    low = (x - high.astype(F32)).astype(BF16)
    return high, low


def symmetrized(tile):
    size = tile.shape[0]
    row = lax.broadcasted_iota(jnp.int32, (size, size), 0) >> 6
    col = lax.broadcasted_iota(jnp.int32, (size, size), 1) >> 6
    tile = tile.astype(F32)
    return jnp.where(row <= col, tile, tile.T).astype(BF16)


def kernel(
    density, pattern_in, out,
    pattern, rows, big, small, wc_hi, wc_lo, big_hi, big_lo, small_hi, small_lo,
    left, middle, square, cube, maskrow,
    pattern_sem, own_sem, pair_send, pair_recv, up_send, down_send, big_recv, fwd_send, fwd_recv, relay_a, relay_b, ready,
):
    wire = lax.axis_index("wire")
    length = lax.axis_size("wire")
    me = lax.axis_index("depth")
    m = me
    half = length // 4
    spot = lax.rem(wire // 2, half)
    h = lax.rem(wire, 2)
    other = wire + 1 - 2 * h
    up = lax.rem(wire - h + 2, length)
    down = lax.rem(wire - h - 1 + length, length)
    source = lax.rem(wire - h + 4 * h - 2 + length, length)

    own = pltpu.make_async_copy(density, rows.at[pl.ds(ROWS * h, ROWS)], own_sem)
    own.start()
    bits_in = pltpu.make_async_copy(pattern_in, pattern, pattern_sem)
    bits_in.start()

    first = spot == 0
    last = spot == half - 1
    seam_left = jnp.logical_and(h == 0, first)
    seam_right = jnp.logical_and(h == 1, last)
    seam = jnp.logical_or(seam_left, seam_right)
    ends = jnp.logical_or(m == 0, m == 5)
    late = 2 * wire >= length
    early = jnp.logical_not(late)
    barrier = pltpu.get_barrier_semaphore()

    def greet(w, d):
        pl.semaphore_signal(barrier, inc=1, device_id={"wire": w, "depth": d}, device_id_type=MESH)

    def when(cond, *more):
        for c in more:
            if c is not True:
                cond = jnp.logical_and(cond, c)
        return pl.when(cond)

    @pl.when(seam)
    def _():
        big[...] = jnp.zeros_like(big)

    greet(other, me)
    expected = jnp.int32(1)

    def counted(cond, n):
        return jnp.where(cond, n, 0)

    @pl.when(jnp.logical_not(seam))
    def _():
        greet(source, me)
        greet(source + 1, me)

    for end, target in ((first, down), (last, up)):
        expected += counted(jnp.logical_not(end), 1)
        expected += counted(jnp.logical_and(end, jnp.logical_and(ends, late)), 1)
    for side, (end, target) in enumerate(((last, up), (first, down))):
        for d, entry in ENTRY[side].items():
            @when(end, early, m == d)
            def _(target=target, entry=entry):
                greet(target, entry)

    for kind, here in enumerate((seam_left, seam_right)):
        for d, entry in ENTRY[kind].items():
            @when(here, early, m == entry)
            def _(d=d):
                greet(source, d)
                greet(source + 1, d)
            expected += counted(jnp.logical_and(jnp.logical_and(here, late), m == entry), 2)
        for giver in range(ROWS):
            for taker in NEXT[kind][giver]:
                asks = (giver, taker) in EARLY_GIVER[kind]
                @when(here, m == (giver if asks else taker))
                def _(peer=taker if asks else giver):
                    greet(wire, peer)
                expected += counted(
                    jnp.logical_and(here, m == (taker if asks else giver)), 1
                )
    pl.semaphore_wait(barrier, expected)

    def is_ready(w, d, slot):
        pl.semaphore_signal(
            ready.at[slot], inc=1, device_id={"wire": w, "depth": d}, device_id_type=MESH
        )

    for kind, here in enumerate((seam_left, seam_right)):
        for d, entry in ENTRY[kind].items():
            @when(here, late, m == entry)
            def _(d=d, kind=kind):
                is_ready(source, d, kind)
                is_ready(source + 1, d, kind)
        for giver in range(ROWS):
            for n, taker in enumerate(NEXT[kind][giver]):
                if (giver, taker) in EARLY_GIVER[kind]:
                    @when(here, m == taker)
                    def _(giver=giver, n=n):
                        is_ready(wire, giver, 2 + n)

    def row_copy(s, t, width, target, depth, sem):
        return pltpu.make_async_remote_copy(
            src_ref=density.at[s, :, pl.ds(DIAG, width)],
            dst_ref=big.at[t, :, pl.ds(0, width)],
            send_sem=sem.at[s], recv_sem=big_recv.at[t],
            device_id={"wire": target, "depth": depth}, device_id_type=MESH,
        )

    def send(act, core, order, target, depth, sem, reach):
        for t in order:
            if t // ROWS == core and t < reach:
                act(row_copy(t % ROWS, t, lanes(reach - t), target, depth, sem))

    def outgoing(act):
        for core in range(2):
            @when(h == core, jnp.logical_not(last))
            def _(core=core):
                send(act, core, NEAR_FIRST, up, me, up_send, CHIP)

            @when(h == core, jnp.logical_not(first))
            def _(core=core):
                send(act, core, NEAR_FIRST, down, me, down_send, CHIP)

    def crossing(act, whose, wait):
        for core in range(2):
            for d, entry in ENTRY[0].items():
                @when(h == core, whose, last, m == d)
                def _(core=core, d=d, entry=entry):
                    if wait:
                        pl.semaphore_wait(ready.at[0], 1)
                    send(act, core, FIRST if d else SECOND, up, entry, up_send, CHIP)

            for d, entry in ENTRY[1].items():
                @when(h == core, whose, first, m == d)
                def _(core=core, d=d, entry=entry):
                    if wait:
                        pl.semaphore_wait(ready.at[1], 1)
                    reach = RIGHT_REACH[2] if d else CHIP
                    send(act, core, NEAR_FIRST, down, entry, down_send, reach)

    def arriving(t, width):
        return row_copy(t % ROWS, t, width, up, me, up_send)

    def relay(t, width, depth, sem):
        return pltpu.make_async_remote_copy(
            src_ref=big.at[t, :, pl.ds(0, width)],
            dst_ref=big.at[t, :, pl.ds(0, width)],
            send_sem=sem.at[t], recv_sem=big_recv.at[t],
            device_id={"wire": wire, "depth": depth}, device_id_type=MESH,
        )

    def forward(s, core):
        width = lanes(ROWS - s)
        return pltpu.make_async_remote_copy(
            src_ref=big.at[ROWS * (1 - core) + s, :, pl.ds(0, width)],
            dst_ref=small.at[s, :, pl.ds(0, width)],
            send_sem=fwd_send.at[s], recv_sem=fwd_recv.at[s],
            device_id={"wire": other}, device_id_type=MESH,
        )

    def hand_on(t, core):
        if t // ROWS == 1 - core:
            forward(t % ROWS, core).start()

    def relays(kind, i):
        if kind == 0:
            for n, (target, which) in enumerate(LEFT_NEXT[i].items()):
                sem = (relay_a, relay_b)[n]
                for t in LEFT_ORDER[i]:
                    if t in which and t in LEFT_ORDER[target]:
                        yield t, relay(t, lanes(CHIP - t), target, sem)
        for target in RIGHT_NEXT[i] if kind else ():
            for t in NEAR_FIRST:
                if t < RIGHT_REACH[target]:
                    yield t, relay(t, lanes(RIGHT_REACH[target] - t), target, relay_a)

    def collect():
        for core in range(2):
            @when(h == core, jnp.logical_not(seam))
            def _(core=core):
                for t in NEAR_FIRST:
                    if t // ROWS == 1 - core:
                        arriving(t, lanes(CHIP - t)).wait_recv()
                        hand_on(t, core)
                for t in NEAR_FIRST:
                    if t // ROWS == core:
                        arriving(t, lanes(CHIP - t)).wait_recv()
        for i in range(ROWS):
            for kind, here in enumerate((seam_left, seam_right)):
                @when(here, m == i)
                def _(i=i, kind=kind):
                    order = NEAR_FIRST if kind else LEFT_ORDER[i]
                    reach = RIGHT_REACH[i] if kind else CHIP
                    onward = list(relays(kind, i))
                    for n, taker in enumerate(NEXT[kind][i]):
                        if (i, taker) in EARLY_GIVER[kind]:
                            pl.semaphore_wait(ready.at[2 + n], 1)
                    for t in order:
                        if t < reach:
                            arriving(t, lanes(reach - t)).wait_recv()
                            for u, copy in onward:
                                if u == t:
                                    copy.start()
                            hand_on(t, kind)

    def drain():
        outgoing(lambda copy: copy.wait_send())
        crossing(lambda copy: copy.wait_send(), True, False)
        pair.wait_send()
        for core in range(2):
            @pl.when(h == core)
            def _(core=core):
                for s in range(ROWS):
                    forward(s, core).wait_send()
        for i in range(ROWS):
            for kind, here in enumerate((seam_left, seam_right)):
                @when(here, m == i)
                def _(i=i, kind=kind):
                    for _, copy in relays(kind, i):
                        copy.wait_send()

    pair = pltpu.make_async_remote_copy(
        src_ref=density, dst_ref=rows.at[pl.ds(ROWS * h, ROWS)],
        send_sem=pair_send, recv_sem=pair_recv,
        device_id={"wire": other}, device_id_type=MESH,
    )
    crossing(lambda copy: copy.start(), late, False)
    outgoing(lambda copy: copy.start())
    pair.start()

    wc_hi[...] = jnp.zeros_like(wc_hi)
    wc_lo[...] = jnp.zeros_like(wc_lo)
    place = ROWS * h + m

    def band_row(index):
        x = rows[index]
        return jnp.concatenate([x, jnp.zeros((ORB, BANDPAD - BAND), F32)], axis=1)

    def build_centre(part):
        for s in range(ROWS):
            x = band_row(ROWS * part + s)
            if s % 2:
                x = pltpu.roll(x, ORB, 1)
            high, low = split(x)
            down_by = pl.ds(pl.multiple_of(part * HALFSIDE + s * ORB, ORB), ORB)
            along = pl.ds(pl.multiple_of(part * HALFSIDE + (s - s % 2) * ORB, 128), BANDPAD)
            wc_hi[down_by, along] = high
            wc_lo[down_by, along] = low

    own.wait()
    build_centre(h)

    def framed(x):
        wide = jnp.concatenate([x, jnp.zeros((x.shape[0], FRAME - BANDPAD), F32)], axis=1)
        return pltpu.roll(wide, place * ORB, 1)

    def stack(ref, x, along):
        high, low = split(x)
        ref[0:ORB, along] = high
        ref[ORB:2 * ORB, along] = low

    stack(left, framed(band_row(place)), slice(0, FRAME))

    bits_in.wait()
    block = lax.broadcasted_iota(jnp.int32, (8, BANDPAD), 1) >> 6
    bits = jnp.zeros((8, BANDPAD), F32)
    for d in range(25):
        bits = jnp.where(block == d, pattern[m, d].astype(F32), bits)
    maskrow[...] = framed(bits)

    def product(ref, along, high, low, across):
        dims = (((1,), (1 if across else 0,)), ((), ()))
        first = lax.dot_general(ref[:, along], high, dims, preferred_element_type=F32)
        second = lax.dot_general(ref[0:ORB, along], low, dims, preferred_element_type=F32)
        return first[0:ORB] + first[ORB:2 * ORB] + second

    def centre(ref, acc):
        for b in range(9):
            a0, a1 = max(0, b - 6), min(3, b + 1)
            down_by = slice(a0 * TILE, a1 * TILE)
            along = slice(b * TILE, (b + 1) * TILE)
            acc[:, along] = product(
                ref, slice(SIDE + a0 * TILE, SIDE + a1 * TILE),
                wc_hi[down_by, along], wc_lo[down_by, along], False,
            )

    def sides(ref, acc):
        for a in range(3):
            down_by = slice(a * TILE, (a + 1) * TILE)
            lo = slice(a * TILE, SIDE)
            hi = slice(2 * SIDE, 2 * SIDE + (a + 1) * TILE)
            acc[:, SIDE + a * TILE:SIDE + (a + 1) * TILE] += (
                product(ref, lo, wc_hi[down_by, lo], wc_lo[down_by, lo], True)
                + product(ref, hi, wc_hi[down_by, hi], wc_lo[down_by, hi], True)
            )

    big_at = h * (2 * SIDE)
    small_at = 2 * SIDE - h * (2 * SIDE - HALFSIDE)

    def corners(ref, acc):
        for b in range(3):
            here = pl.ds(pl.multiple_of(big_at + b * TILE, 128), TILE)
            upto = (b + 1) * TILE
            total = product(
                ref, pl.ds(pl.multiple_of(big_at, 128), upto),
                big_hi[0:upto, b * TILE:upto], big_lo[0:upto, b * TILE:upto], False,
            )
            if b < 2:
                total += product(
                    ref, pl.ds(pl.multiple_of(big_at + upto, 128), SIDE - upto),
                    big_hi[b * TILE:upto, upto:SIDE], big_lo[b * TILE:upto, upto:SIDE], True,
                )
            acc[:, here] += total
        here = pl.ds(pl.multiple_of(small_at, 128), HALFSIDE)
        acc[:, here] += product(ref, here, small_hi[...], small_lo[...], False)

    pair.wait_recv()
    build_centre(1 - h)

    centre(left, square)
    sides(left, square)
    mid = slice(SIDE, 2 * SIDE)
    masked = square[:, mid] * maskrow[0:1, mid]
    square[:, mid] = masked
    stack(middle, masked, mid)
    centre(middle, cube)

    crossing(lambda copy: copy.start(), early, True)
    collect()

    def build_triangle(source_ref, high_ref, low_ref, count):
        for t in range(count):
            x = source_ref[t, :, 0:lanes(count - t)]
            if t % 2:
                x = pltpu.roll(x, ORB, 1)
                lane = lax.broadcasted_iota(jnp.int32, x.shape, 1)
                x = jnp.where(lane < ORB, 0.0, x)
            high, low = split(x)
            along = slice((t - t % 2) * ORB, count * ORB)
            high_ref[t * ORB:(t + 1) * ORB, along] = high
            low_ref[t * ORB:(t + 1) * ORB, along] = low

    build_triangle(big, big_hi, big_lo, CHIP)
    for ref in (big_hi, big_lo):
        for a in range(3):
            tile = slice(a * TILE, (a + 1) * TILE)
            ref[tile, tile] = symmetrized(ref[tile, tile])
    for s in range(ROWS):
        forward(s, 0).wait_recv()
    build_triangle(small, small_hi, small_lo, ROWS)
    for ref in (small_hi, small_lo):
        ref[...] = symmetrized(ref[...])

    corners(left, square)
    for along in (slice(0, SIDE), slice(2 * SIDE, FRAME)):
        masked = square[:, along] * maskrow[0:1, along]
        square[:, along] = masked
        stack(middle, masked, along)
    sides(middle, cube)
    corners(middle, cube)

    result = 3.0 * square[...] - 2.0 * (cube[...] * maskrow[0:1, :])
    out[0] = pltpu.roll(result, FRAME - place * ORB, 1)[:, 0:BAND]

    drain()


def on_device(density, pattern):
    dma = pltpu.SemaphoreType.DMA
    return pl.pallas_call(
        kernel,
        out_shape=jax.ShapeDtypeStruct((1, ORB, BAND), F32),
        in_specs=[pl.BlockSpec(memory_space=pltpu.HBM)] * 2,
        out_specs=pl.BlockSpec(memory_space=pltpu.VMEM),
        scratch_shapes=[
            pltpu.SMEM((ROWS, 25), jnp.int32),
            pltpu.VMEM((CHIP, ORB, BAND), F32),
            pltpu.VMEM((CHIP, ORB, SIDE), F32),
            pltpu.VMEM((ROWS, ORB, HALFSIDE), F32),
            pltpu.VMEM((SIDE, FRAME), BF16),
            pltpu.VMEM((SIDE, FRAME), BF16),
            pltpu.VMEM((SIDE, SIDE), BF16),
            pltpu.VMEM((SIDE, SIDE), BF16),
            pltpu.VMEM((HALFSIDE, HALFSIDE), BF16),
            pltpu.VMEM((HALFSIDE, HALFSIDE), BF16),
            pltpu.VMEM((2 * ORB, FRAME), BF16),
            pltpu.VMEM((2 * ORB, FRAME), BF16),
            pltpu.VMEM((ORB, FRAME), F32),
            pltpu.VMEM((ORB, FRAME), F32),
            pltpu.VMEM((8, FRAME), F32),
            dma, dma, dma, dma, dma((ROWS,)), dma((ROWS,)), dma((CHIP,)), dma((ROWS,)), dma((ROWS,)),
            dma((CHIP,)), dma((CHIP,)), pltpu.SemaphoreType.REGULAR((4,)),
        ],
        compiler_params=pltpu.CompilerParams(
            collective_id=0, has_side_effects=True, vmem_limit_bytes=62 * 1024 * 1024
        ),
    )(density, pattern)


def solution(mesh):
    in_specs = (P("wire", None, None), P("wire", None))
    out_specs = P(("wire", "depth"), None, None)
    return jax.shard_map(
        on_device, mesh=mesh, in_specs=in_specs, out_specs=out_specs, check_vma=False
    )
```

```python
import jax
import jax.numpy as jnp
from jax import lax
from jax.experimental import pallas as pl
from jax.experimental.pallas import tpu as pltpu
from jax.sharding import PartitionSpec as P

MESH = pl.DeviceIdType.MESH
ORB = 64
ROWS = 6
CHIP = 2 * ROWS
PIECES = 3 * ROWS
FRAME = 3 * CHIP * ORB
SIDE = CHIP * ORB
HALFSIDE = ROWS * ORB
BAND = 25 * ORB
BANDPAD = 26 * ORB
TILE = 256
DIAG = 12 * ORB
F32 = jnp.float32
VMEM_LIMIT = 63200 * 1024
BF16 = jnp.bfloat16


FIRST = (8, 10, 5, 2, 1)
SECOND = (6, 3, 7, 9, 4, 11)
COMMON = (6, 8, 7, 5, 9, 10, 11)
LEFT_ORDER = (
    (8, 10, 6, 7, 9, 11, 5, 2, 3, 1, 4, 0),
    (8, 10, 5, 2, 6, 3, 1, 7, 9, 4, 11),
    (6, 3, 7, 9, 4, 11, 8, 10, 5, 2),
    (6, 3, 7, 9, 4, 11, 8, 10, 5),
    (4, *COMMON),
    COMMON,
)
LEFT_NEXT = (
    {},
    {2: (8, 10, 5, 2), 3: (8, 10, 5), 0: (*FIRST, 3, 4)},
    {1: SECOND, 3: SECOND, 4: (4,), 0: (6, 7, 9, 11)},
    {},
    {},
    {4: COMMON},
)
RIGHT_REACH = (7, 9, 9, 10, 12, 12)
RIGHT_NEXT = ((), (0, 2), (), (), (3, 5), ())
NEXT = (LEFT_NEXT, RIGHT_NEXT)
ORDER = (
    (6, 0, 7, 8, 1, 9, 10, 11, 2, 3, 4, 5),
    (6, 0, 1, 7, 2, 8, 3, 9, 4, 10, 5, 11, 12, 13, 14, 15, 16, 17),
)
ENTRY = (
    ((5, 1, FIRST), (5, 0, (0,)), (0, 2, SECOND), (0, 5, COMMON)),
    ((5, 1, ORDER[1]), (0, 4, ORDER[1])),
)
EARLY_GIVER = (((1, 2), (1, 3), (1, 0), (2, 3), (2, 4)), ((1, 2), (4, 5)))
EARLY_SLOT = (2, 3, 4, 5)
SLOTS = 6


def row_of(p):
    return p % CHIP


def core_of(p):
    return row_of(p) // ROWS


def cores_of(order):
    return sorted({core_of(p) for p in order})


def lanes(blocks):
    return (blocks + 1) // 2 * 2 * ORB


def split(x):
    high = x.astype(BF16)
    low = (x - high.astype(F32)).astype(BF16)
    return high, low


def symmetrized(tile):
    size = tile.shape[0]
    row = lax.broadcasted_iota(jnp.int32, (size, size), 0) >> 6
    col = lax.broadcasted_iota(jnp.int32, (size, size), 1) >> 6
    tile = tile.astype(F32)
    return jnp.where(row <= col, tile, tile.T).astype(BF16)


def kernel(
    density, pattern_in, out,
    pattern, rows, big, small, wc_hi, wc_lo, big_hi, big_lo, small_hi, small_lo,
    left, middle, square, cube, maskrow,
    pattern_sem, own_sem, pair_send, pair_recv, up_send, down_send, big_recv, fwd_send, fwd_recv, relay_send, ready,
):
    wire = lax.axis_index("wire")
    length = lax.axis_size("wire")
    me = lax.axis_index("depth")
    m = me
    half = length // 4
    spot = lax.rem(wire // 2, half)
    h = lax.rem(wire, 2)
    other = wire + 1 - 2 * h
    up = lax.rem(wire - h + 2, length)
    down = lax.rem(wire - h - 1 + length, length)
    source = lax.rem(wire - h + 4 * h - 2 + length, length)

    own = pltpu.make_async_copy(density, rows.at[pl.ds(ROWS * h, ROWS)], own_sem)
    own.start()
    bits_in = pltpu.make_async_copy(pattern_in, pattern, pattern_sem)
    bits_in.start()

    first = spot == 0
    last = spot == half - 1
    seam_left = jnp.logical_and(h == 0, first)
    seam_right = jnp.logical_and(h == 1, last)
    seam = jnp.logical_or(seam_left, seam_right)
    ends = jnp.logical_or(m == 0, m == 5)
    late = 2 * wire >= length
    early = jnp.logical_not(late)
    barrier = pltpu.get_barrier_semaphore()

    def greet(w, d):
        pl.semaphore_signal(barrier, inc=1, device_id={"wire": w, "depth": d}, device_id_type=MESH)

    def when(cond, *more):
        for c in more:
            if c is not True:
                cond = jnp.logical_and(cond, c)
        return pl.when(cond)

    @pl.when(seam)
    def _():
        big[...] = jnp.zeros_like(big)

    greet(other, me)
    expected = jnp.int32(1)

    def counted(cond, n):
        return jnp.where(cond, n, 0)

    @pl.when(jnp.logical_not(seam))
    def _():
        greet(source, me)
        greet(source + 1, me)

    expected += counted(jnp.logical_not(first), 1) + counted(jnp.logical_not(last), 1)
    entries = [
        (slot, kind, (last, first)[kind], (up, down)[kind], (seam_left, seam_right)[kind], *entry)
        for slot, (kind, entry) in enumerate((k, e) for k in range(2) for e in ENTRY[k])
    ]
    for slot, kind, end, target, here, giver, taker, order in entries:
        for core in cores_of(order):
            gives = jnp.logical_and(jnp.logical_and(end, h == core), m == giver)
            takes = jnp.logical_and(here, m == taker)
            if slot in EARLY_SLOT:
                expected += counted(jnp.logical_and(gives, late), 1)
                expected += counted(jnp.logical_and(takes, late), 1)

                @when(gives, early)
                def _(target=target, taker=taker):
                    greet(target, taker)
            else:
                expected += counted(gives, 1)

            @when(takes, early if slot in EARLY_SLOT else True)
            def _(giver=giver, core=core):
                greet(source + core, giver)

    for kind, here in enumerate((seam_left, seam_right)):
        for giver in range(ROWS):
            for taker in NEXT[kind][giver]:
                asks = (giver, taker) in EARLY_GIVER[kind]
                @when(here, m == (giver if asks else taker))
                def _(peer=taker if asks else giver):
                    greet(wire, peer)
                expected += counted(
                    jnp.logical_and(here, m == (taker if asks else giver)), 1
                )
    pl.semaphore_wait(barrier, expected)

    def is_ready(w, d, slot):
        pl.semaphore_signal(
            ready.at[slot], inc=1, device_id={"wire": w, "depth": d}, device_id_type=MESH
        )

    for slot, kind, end, target, here, giver, taker, order in entries:
        for core in cores_of(order) if slot in EARLY_SLOT else ():
            @when(here, late, m == taker)
            def _(giver=giver, core=core, slot=slot):
                is_ready(source + core, giver, slot)

    for kind, here in enumerate((seam_left, seam_right)):
        for giver in range(ROWS):
            for n, taker in enumerate(NEXT[kind][giver]):
                if (giver, taker) in EARLY_GIVER[kind]:
                    @when(here, m == taker)
                    def _(giver=giver, n=n):
                        is_ready(wire, giver, SLOTS + n)

    def part(kind, p, reach):
        t = row_of(p)
        if kind == 0 or t >= ROWS:
            return t, 0, lanes(reach - t)
        near = lanes(ROWS - t)
        return (t, 0, near) if p < CHIP else (t, near, lanes(reach - t) - near)

    def row_copy(kind, p, reach, target, depth, second=0):
        t, start, width = part(kind, p, reach)
        sem = down_send.at[t % ROWS + p // CHIP * ROWS] if kind else up_send.at[t % ROWS + second * ROWS]
        return pltpu.make_async_remote_copy(
            src_ref=density.at[t % ROWS, :, pl.ds(DIAG + start, width)],
            dst_ref=big.at[t, :, pl.ds(start, width)],
            send_sem=sem, recv_sem=big_recv.at[p],
            device_id={"wire": target, "depth": depth}, device_id_type=MESH,
        )

    def present(kind, p, reach):
        return row_of(p) < reach and part(kind, p, reach)[2] > 0

    def send(act, kind, core, order, target, depth, reach, second=0):
        for p in order:
            if core_of(p) == core and present(kind, p, reach):
                act(row_copy(kind, p, reach, target, depth, second))

    def outgoing(act):
        for core in range(2):
            @when(h == core, jnp.logical_not(first))
            def _(core=core):
                send(act, 1, core, ORDER[1][:CHIP], down, me, CHIP)

            @when(h == core, jnp.logical_not(last))
            def _(core=core):
                send(act, 0, core, ORDER[0], up, me, CHIP)

            @when(h == core, jnp.logical_not(first))
            def _(core=core):
                send(act, 1, core, ORDER[1][CHIP:], down, me, CHIP)

    def crossing(act, whose, deferred, wait):
        for slot, kind, end, target, here, giver, taker, order in entries:
            if deferred and slot not in EARLY_SLOT:
                continue
            for core in cores_of(order):
                @when(h == core, whose if slot in EARLY_SLOT else True, end, m == giver)
                def _(core=core, slot=slot, kind=kind, target=target, taker=taker, order=order):
                    if wait:
                        pl.semaphore_wait(ready.at[slot], 1)
                    reach = RIGHT_REACH[taker] if kind else CHIP
                    send(act, kind, core, order, target, taker, reach, slot == 3)

    def arriving(kind, p, reach):
        return row_copy(kind, p, reach, up, me)

    def relay(kind, p, reach, depth, n):
        t, start, width = part(kind, p, reach)
        return pltpu.make_async_remote_copy(
            src_ref=big.at[t, :, pl.ds(start, width)],
            dst_ref=big.at[t, :, pl.ds(start, width)],
            send_sem=relay_send.at[n, p], recv_sem=big_recv.at[p],
            device_id={"wire": wire, "depth": depth}, device_id_type=MESH,
        )

    def forward(s, core):
        width = lanes(ROWS - s)
        return pltpu.make_async_remote_copy(
            src_ref=big.at[ROWS * (1 - core) + s, :, pl.ds(0, width)],
            dst_ref=small.at[s, :, pl.ds(0, width)],
            send_sem=fwd_send.at[s], recv_sem=fwd_recv.at[s],
            device_id={"wire": other}, device_id_type=MESH,
        )

    def hand_on(p, core):
        if p < CHIP and core_of(p) == 1 - core:
            forward(p % ROWS, core).start()

    def relays(kind, i):
        if kind == 0:
            for n, (target, which) in enumerate(LEFT_NEXT[i].items()):
                for p in LEFT_ORDER[i]:
                    if p in which and p in LEFT_ORDER[target]:
                        yield p, relay(0, p, CHIP, target, n)
        for n, target in enumerate(RIGHT_NEXT[i] if kind else ()):
            for p in ORDER[1]:
                if present(1, p, RIGHT_REACH[target]):
                    yield p, relay(1, p, RIGHT_REACH[target], target, n)

    def collect():
        for core in range(2):
            @when(h == core, jnp.logical_not(seam))
            def _(core=core):
                for near in (True, False):
                    for p in ORDER[core]:
                        if (p < CHIP and core_of(p) == 1 - core) == near:
                            arriving(core, p, CHIP).wait_recv()
                            hand_on(p, core)
        for i in range(ROWS):
            for kind, here in enumerate((seam_left, seam_right)):
                @when(here, m == i)
                def _(i=i, kind=kind):
                    order = ORDER[1] if kind else LEFT_ORDER[i]
                    reach = RIGHT_REACH[i] if kind else CHIP
                    onward = list(relays(kind, i))
                    for n, taker in enumerate(NEXT[kind][i]):
                        if (i, taker) in EARLY_GIVER[kind]:
                            pl.semaphore_wait(ready.at[SLOTS + n], 1)
                    for p in order:
                        if present(kind, p, reach):
                            arriving(kind, p, reach).wait_recv()
                            for q, copy in onward:
                                if q == p:
                                    copy.start()
                            hand_on(p, kind)

    def drain():
        outgoing(lambda copy: copy.wait_send())
        crossing(lambda copy: copy.wait_send(), True, False, False)
        pair.wait_send()
        for core in range(2):
            @pl.when(h == core)
            def _(core=core):
                for s in range(ROWS):
                    forward(s, core).wait_send()
        for i in range(ROWS):
            for kind, here in enumerate((seam_left, seam_right)):
                @when(here, m == i)
                def _(i=i, kind=kind):
                    for _, copy in relays(kind, i):
                        copy.wait_send()

    pair = pltpu.make_async_remote_copy(
        src_ref=density, dst_ref=rows.at[pl.ds(ROWS * h, ROWS)],
        send_sem=pair_send, recv_sem=pair_recv,
        device_id={"wire": other}, device_id_type=MESH,
    )
    crossing(lambda copy: copy.start(), late, False, False)
    outgoing(lambda copy: copy.start())
    pair.start()

    wc_hi[...] = jnp.zeros_like(wc_hi)
    wc_lo[...] = jnp.zeros_like(wc_lo)
    place = ROWS * h + m

    def band_row(index):
        x = rows[index]
        return jnp.concatenate([x, jnp.zeros((ORB, BANDPAD - BAND), F32)], axis=1)

    def build_centre(part):
        for s in range(ROWS):
            x = band_row(ROWS * part + s)
            if s % 2:
                x = pltpu.roll(x, ORB, 1)
            high, low = split(x)
            down_by = pl.ds(pl.multiple_of(part * HALFSIDE + s * ORB, ORB), ORB)
            along = pl.ds(pl.multiple_of(part * HALFSIDE + (s - s % 2) * ORB, 128), BANDPAD)
            wc_hi[down_by, along] = high
            wc_lo[down_by, along] = low

    own.wait()
    build_centre(h)

    def framed(x):
        wide = jnp.concatenate([x, jnp.zeros((x.shape[0], FRAME - BANDPAD), F32)], axis=1)
        return pltpu.roll(wide, place * ORB, 1)

    def stack(ref, x, along):
        high, low = split(x)
        ref[0:ORB, along] = high
        ref[ORB:2 * ORB, along] = low

    stack(left, framed(band_row(place)), slice(0, FRAME))

    bits_in.wait()
    block = lax.broadcasted_iota(jnp.int32, (8, BANDPAD), 1) >> 6
    bits = jnp.zeros((8, BANDPAD), F32)
    for d in range(25):
        bits = jnp.where(block == d, pattern[m, d].astype(F32), bits)
    maskrow[...] = framed(bits)

    def product(ref, along, high, low, across):
        dims = (((1,), (1 if across else 0,)), ((), ()))
        first = lax.dot_general(ref[:, along], high, dims, preferred_element_type=F32)
        second = lax.dot_general(ref[0:ORB, along], low, dims, preferred_element_type=F32)
        return first[0:ORB] + first[ORB:2 * ORB] + second

    def centre(ref, acc):
        for b in range(9):
            a0, a1 = max(0, b - 6), min(3, b + 1)
            down_by = slice(a0 * TILE, a1 * TILE)
            along = slice(b * TILE, (b + 1) * TILE)
            acc[:, along] = product(
                ref, slice(SIDE + a0 * TILE, SIDE + a1 * TILE),
                wc_hi[down_by, along], wc_lo[down_by, along], False,
            )

    def sides(ref, acc):
        for a in range(3):
            down_by = slice(a * TILE, (a + 1) * TILE)
            lo = slice(a * TILE, SIDE)
            hi = slice(2 * SIDE, 2 * SIDE + (a + 1) * TILE)
            acc[:, SIDE + a * TILE:SIDE + (a + 1) * TILE] += (
                product(ref, lo, wc_hi[down_by, lo], wc_lo[down_by, lo], True)
                + product(ref, hi, wc_hi[down_by, hi], wc_lo[down_by, hi], True)
            )

    big_at = h * (2 * SIDE)
    small_at = 2 * SIDE - h * (2 * SIDE - HALFSIDE)

    def corners(ref, acc):
        for b in range(3):
            here = pl.ds(pl.multiple_of(big_at + b * TILE, 128), TILE)
            upto = (b + 1) * TILE
            total = product(
                ref, pl.ds(pl.multiple_of(big_at, 128), upto),
                big_hi[0:upto, b * TILE:upto], big_lo[0:upto, b * TILE:upto], False,
            )
            if b < 2:
                total += product(
                    ref, pl.ds(pl.multiple_of(big_at + upto, 128), SIDE - upto),
                    big_hi[b * TILE:upto, upto:SIDE], big_lo[b * TILE:upto, upto:SIDE], True,
                )
            acc[:, here] += total
        here = pl.ds(pl.multiple_of(small_at, 128), HALFSIDE)
        acc[:, here] += product(ref, here, small_hi[...], small_lo[...], False)

    pair.wait_recv()
    build_centre(1 - h)

    centre(left, square)
    sides(left, square)
    mid = slice(SIDE, 2 * SIDE)
    masked = square[:, mid] * maskrow[0:1, mid]
    square[:, mid] = masked
    stack(middle, masked, mid)
    centre(middle, cube)

    crossing(lambda copy: copy.start(), early, True, True)
    collect()

    def build_triangle(source_ref, high_ref, low_ref, count):
        for t in range(count):
            x = source_ref[t, :, 0:lanes(count - t)]
            if t % 2:
                x = pltpu.roll(x, ORB, 1)
                lane = lax.broadcasted_iota(jnp.int32, x.shape, 1)
                x = jnp.where(lane < ORB, 0.0, x)
            high, low = split(x)
            along = slice((t - t % 2) * ORB, count * ORB)
            high_ref[t * ORB:(t + 1) * ORB, along] = high
            low_ref[t * ORB:(t + 1) * ORB, along] = low

    build_triangle(big, big_hi, big_lo, CHIP)
    for ref in (big_hi, big_lo):
        for a in range(3):
            tile = slice(a * TILE, (a + 1) * TILE)
            ref[tile, tile] = symmetrized(ref[tile, tile])
    for s in range(ROWS):
        forward(s, 0).wait_recv()
    build_triangle(small, small_hi, small_lo, ROWS)
    for ref in (small_hi, small_lo):
        ref[...] = symmetrized(ref[...])

    corners(left, square)
    for along in (slice(0, SIDE), slice(2 * SIDE, FRAME)):
        masked = square[:, along] * maskrow[0:1, along]
        square[:, along] = masked
        stack(middle, masked, along)
    sides(middle, cube)
    corners(middle, cube)

    result = 3.0 * square[...] - 2.0 * (cube[...] * maskrow[0:1, :])
    out[0] = pltpu.roll(result, FRAME - place * ORB, 1)[:, 0:BAND]

    drain()


def on_device(density, pattern):
    dma = pltpu.SemaphoreType.DMA
    return pl.pallas_call(
        kernel,
        out_shape=jax.ShapeDtypeStruct((1, ORB, BAND), F32),
        in_specs=[pl.BlockSpec(memory_space=pltpu.HBM)] * 2,
        out_specs=pl.BlockSpec(memory_space=pltpu.VMEM),
        scratch_shapes=[
            pltpu.SMEM((ROWS, 25), jnp.int32),
            pltpu.VMEM((CHIP, ORB, BAND), F32),
            pltpu.VMEM((CHIP, ORB, SIDE), F32),
            pltpu.VMEM((ROWS, ORB, HALFSIDE), F32),
            pltpu.VMEM((SIDE, FRAME), BF16),
            pltpu.VMEM((SIDE, FRAME), BF16),
            pltpu.VMEM((SIDE, SIDE), BF16),
            pltpu.VMEM((SIDE, SIDE), BF16),
            pltpu.VMEM((HALFSIDE, HALFSIDE), BF16),
            pltpu.VMEM((HALFSIDE, HALFSIDE), BF16),
            pltpu.VMEM((2 * ORB, FRAME), BF16),
            pltpu.VMEM((2 * ORB, FRAME), BF16),
            pltpu.VMEM((ORB, FRAME), F32),
            pltpu.VMEM((ORB, FRAME), F32),
            pltpu.VMEM((8, FRAME), F32),
            dma, dma, dma, dma, dma((CHIP,)), dma((CHIP,)), dma((PIECES,)), dma((ROWS,)), dma((ROWS,)),
            dma((4, PIECES)), pltpu.SemaphoreType.REGULAR((SLOTS + 4,)),
        ],
        compiler_params=pltpu.CompilerParams(
            collective_id=0, has_side_effects=True, vmem_limit_bytes=VMEM_LIMIT
        ),
    )(density, pattern)


def solution(mesh):
    in_specs = (P("wire", None, None), P("wire", None))
    out_specs = P(("wire", "depth"), None, None)
    return jax.shard_map(
        on_device, mesh=mesh, in_specs=in_specs, out_specs=out_specs, check_vma=False
    )
```

```python
import jax
import jax.numpy as jnp
from jax import lax
from jax.experimental import pallas as pl
from jax.experimental.pallas import tpu as pltpu
from jax.sharding import PartitionSpec as P

MESH = pl.DeviceIdType.MESH
ORB = 64
ROWS = 6
CHIP = 2 * ROWS
PIECES = 3 * ROWS
FRAME = 3 * CHIP * ORB
SIDE = CHIP * ORB
HALFSIDE = ROWS * ORB
BAND = 25 * ORB
BANDPAD = 26 * ORB
TILE = 256
DIAG = 12 * ORB
F32 = jnp.float32
VMEM_LIMIT = 54000 * 1024
BF16 = jnp.bfloat16


FIRST = (8, 10, 5, 2, 1)
SECOND = (6, 7, 3, 9, 11, 4)
COMMON = (6, 8, 7, 5, 9, 10, 11)
LEFT_ORDER = (
    (8, 10, 6, 7, 9, 11, 5, 2, 3, 4, 1, 0),
    (8, 10, 5, 2, 6, 7, 3, 1, 9, 11, 4),
    (6, 7, 3, 9, 11, 4, 8, 10, 5, 2),
    (6, 7, 3, 9, 11, 4, 8, 10, 5),
    (4, *COMMON),
    COMMON,
)
LEFT_NEXT = (
    {},
    {2: (8, 10, 5, 2), 3: (8, 10, 5), 0: (8, 10, 5, 2, 3, 4)},
    {1: SECOND, 3: SECOND, 4: (4,), 0: (6, 7, 9, 11)},
    {},
    {},
    {4: COMMON},
)
RIGHT_REACH = (7, 9, 9, 10, 12, 12)
RIGHT_NEXT = ((), (0, 2), (), (), (3, 5), ())
NEXT = (LEFT_NEXT, RIGHT_NEXT)
ORDER = (
    (6, 0, 7, 8, 1, 9, 10, 11, 2, 3, 4, 5),
    (6, 0, 1, 7, 2, 8, 3, 9, 4, 10, 5, 11, 12, 13, 14, 15, 16, 17),
)
ENTRY = (
    ((5, 1, FIRST), (5, 0, (1, 0)), (0, 2, SECOND), (0, 5, COMMON)),
    ((5, 1, ORDER[1]), (0, 4, ORDER[1])),
)
EARLY_GIVER = (((1, 2), (1, 3), (1, 0), (2, 3), (2, 4)), ((1, 2), (4, 5)))
EARLY_SLOT = (2, 3, 4, 5)
SLOTS = 6


def row_of(p):
    return p % CHIP


def core_of(p):
    return row_of(p) // ROWS


def cores_of(order):
    return sorted({core_of(p) for p in order})


def lanes(blocks):
    return (blocks + 1) // 2 * 2 * ORB


def split(x):
    high = x.astype(BF16)
    low = (x - high.astype(F32)).astype(BF16)
    return high, low


def symmetrized(tile):
    size = tile.shape[0]
    row = lax.broadcasted_iota(jnp.int32, (size, size), 0) >> 6
    col = lax.broadcasted_iota(jnp.int32, (size, size), 1) >> 6
    tile = tile.astype(F32)
    return jnp.where(row <= col, tile, tile.T).astype(BF16)


def kernel(
    density, pattern_in, out,
    pattern, rows, big, small, wc_hi, wc_lo, big_hi, big_lo, small_hi, small_lo,
    left, middle, square, cube, maskrow,
    pattern_sem, own_sem, pair_send, pair_recv, up_send, down_send, big_recv, fwd_send, fwd_recv, relay_send, ready,
):
    wire = lax.axis_index("wire")
    length = lax.axis_size("wire")
    me = lax.axis_index("depth")
    m = me
    half = length // 4
    spot = lax.rem(wire // 2, half)
    h = lax.rem(wire, 2)
    other = wire + 1 - 2 * h
    up = lax.rem(wire - h + 2, length)
    down = lax.rem(wire - h - 1 + length, length)
    source = lax.rem(wire - h + 4 * h - 2 + length, length)

    own = pltpu.make_async_copy(density, rows.at[pl.ds(ROWS * h, ROWS)], own_sem)
    own.start()
    bits_in = pltpu.make_async_copy(pattern_in, pattern, pattern_sem)
    bits_in.start()

    first = spot == 0
    last = spot == half - 1
    seam_left = jnp.logical_and(h == 0, first)
    seam_right = jnp.logical_and(h == 1, last)
    seam = jnp.logical_or(seam_left, seam_right)
    ends = jnp.logical_or(m == 0, m == 5)
    late = 2 * wire >= length
    early = jnp.logical_not(late)
    barrier = pltpu.get_barrier_semaphore()

    def greet(w, d):
        pl.semaphore_signal(barrier, inc=1, device_id={"wire": w, "depth": d}, device_id_type=MESH)

    def when(cond, *more):
        for c in more:
            if c is not True:
                cond = jnp.logical_and(cond, c)
        return pl.when(cond)

    @pl.when(seam)
    def _():
        big[...] = jnp.zeros_like(big)

    greet(other, me)
    expected = jnp.int32(1)

    def counted(cond, n):
        return jnp.where(cond, n, 0)

    @pl.when(jnp.logical_not(seam))
    def _():
        greet(source, me)
        greet(source + 1, me)

    expected += counted(jnp.logical_not(first), 1) + counted(jnp.logical_not(last), 1)
    entries = [
        (slot, kind, (last, first)[kind], (up, down)[kind], (seam_left, seam_right)[kind], *entry)
        for slot, (kind, entry) in enumerate((k, e) for k in range(2) for e in ENTRY[k])
    ]
    for slot, kind, end, target, here, giver, taker, order in entries:
        for core in cores_of(order):
            gives = jnp.logical_and(jnp.logical_and(end, h == core), m == giver)
            takes = jnp.logical_and(here, m == taker)
            if slot in EARLY_SLOT:
                expected += counted(jnp.logical_and(gives, late), 1)
                expected += counted(jnp.logical_and(takes, late), 1)

                @when(gives, early)
                def _(target=target, taker=taker):
                    greet(target, taker)
            else:
                expected += counted(gives, 1)

            @when(takes, early if slot in EARLY_SLOT else True)
            def _(giver=giver, core=core):
                greet(source + core, giver)

    for kind, here in enumerate((seam_left, seam_right)):
        for giver in range(ROWS):
            for taker in NEXT[kind][giver]:
                asks = (giver, taker) in EARLY_GIVER[kind]
                @when(here, m == (giver if asks else taker))
                def _(peer=taker if asks else giver):
                    greet(wire, peer)
                expected += counted(
                    jnp.logical_and(here, m == (taker if asks else giver)), 1
                )
    pl.semaphore_wait(barrier, expected)

    def is_ready(w, d, slot):
        pl.semaphore_signal(
            ready.at[slot], inc=1, device_id={"wire": w, "depth": d}, device_id_type=MESH
        )

    for slot, kind, end, target, here, giver, taker, order in entries:
        for core in cores_of(order) if slot in EARLY_SLOT else ():
            @when(here, late, m == taker)
            def _(giver=giver, core=core, slot=slot):
                is_ready(source + core, giver, slot)

    for kind, here in enumerate((seam_left, seam_right)):
        for giver in range(ROWS):
            for n, taker in enumerate(NEXT[kind][giver]):
                if (giver, taker) in EARLY_GIVER[kind]:
                    @when(here, m == taker)
                    def _(giver=giver, n=n):
                        is_ready(wire, giver, SLOTS + n)

    def part(kind, p, reach):
        t = row_of(p)
        if kind == 0 or t >= ROWS:
            return t, 0, lanes(reach - t)
        near = lanes(ROWS - t)
        return (t, 0, near) if p < CHIP else (t, near, lanes(reach - t) - near)

    def row_copy(kind, p, reach, target, depth, second=0):
        t, start, width = part(kind, p, reach)
        sem = down_send.at[t % ROWS + p // CHIP * ROWS] if kind else up_send.at[t % ROWS + second * ROWS]
        return pltpu.make_async_remote_copy(
            src_ref=density.at[t % ROWS, :, pl.ds(DIAG + start, width)],
            dst_ref=big.at[t, :, pl.ds(start, width)],
            send_sem=sem, recv_sem=big_recv.at[p],
            device_id={"wire": target, "depth": depth}, device_id_type=MESH,
        )

    def present(kind, p, reach):
        return row_of(p) < reach and part(kind, p, reach)[2] > 0

    def send(act, kind, core, order, target, depth, reach, second=0):
        for p in order:
            if core_of(p) == core and present(kind, p, reach):
                act(row_copy(kind, p, reach, target, depth, second))

    def outgoing(act):
        for core in range(2):
            @when(h == core, jnp.logical_not(first))
            def _(core=core):
                send(act, 1, core, ORDER[1][:CHIP], down, me, CHIP)

            @when(h == core, jnp.logical_not(last))
            def _(core=core):
                send(act, 0, core, ORDER[0], up, me, CHIP)

            @when(h == core, jnp.logical_not(first))
            def _(core=core):
                send(act, 1, core, ORDER[1][CHIP:], down, me, CHIP)

    def crossing(act, whose, deferred, wait):
        for slot, kind, end, target, here, giver, taker, order in entries:
            if deferred and slot not in EARLY_SLOT:
                continue
            for core in cores_of(order):
                @when(h == core, whose if slot in EARLY_SLOT else True, end, m == giver)
                def _(core=core, slot=slot, kind=kind, target=target, taker=taker, order=order):
                    if wait:
                        pl.semaphore_wait(ready.at[slot], 1)
                    reach = RIGHT_REACH[taker] if kind else CHIP
                    send(act, kind, core, order, target, taker, reach, slot in (1, 3))

    def arriving(kind, p, reach):
        return row_copy(kind, p, reach, up, me)

    def relay(kind, p, reach, depth, n):
        t, start, width = part(kind, p, reach)
        return pltpu.make_async_remote_copy(
            src_ref=big.at[t, :, pl.ds(start, width)],
            dst_ref=big.at[t, :, pl.ds(start, width)],
            send_sem=relay_send.at[n, p], recv_sem=big_recv.at[p],
            device_id={"wire": wire, "depth": depth}, device_id_type=MESH,
        )

    def forward(s, core):
        width = lanes(ROWS - s)
        return pltpu.make_async_remote_copy(
            src_ref=big.at[ROWS * (1 - core) + s, :, pl.ds(0, width)],
            dst_ref=small.at[s, :, pl.ds(0, width)],
            send_sem=fwd_send.at[s], recv_sem=fwd_recv.at[s],
            device_id={"wire": other}, device_id_type=MESH,
        )

    def hand_on(p, core):
        if p < CHIP and core_of(p) == 1 - core:
            forward(p % ROWS, core).start()

    def relays(kind, i):
        if kind == 0:
            for n, (target, which) in enumerate(LEFT_NEXT[i].items()):
                for p in LEFT_ORDER[i]:
                    if p in which and p in LEFT_ORDER[target]:
                        yield p, relay(0, p, CHIP, target, n)
        for n, target in enumerate(RIGHT_NEXT[i] if kind else ()):
            for p in ORDER[1]:
                if present(1, p, RIGHT_REACH[target]):
                    yield p, relay(1, p, RIGHT_REACH[target], target, n)

    def collect():
        for core in range(2):
            @when(h == core, jnp.logical_not(seam))
            def _(core=core):
                for near in (True, False):
                    for p in ORDER[core]:
                        if (p < CHIP and core_of(p) == 1 - core) == near:
                            arriving(core, p, CHIP).wait_recv()
                            hand_on(p, core)
        for i in range(ROWS):
            for kind, here in enumerate((seam_left, seam_right)):
                @when(here, m == i)
                def _(i=i, kind=kind):
                    order = ORDER[1] if kind else LEFT_ORDER[i]
                    reach = RIGHT_REACH[i] if kind else CHIP
                    onward = list(relays(kind, i))
                    for n, taker in enumerate(NEXT[kind][i]):
                        if (i, taker) in EARLY_GIVER[kind]:
                            pl.semaphore_wait(ready.at[SLOTS + n], 1)
                    for p in order:
                        if present(kind, p, reach):
                            arriving(kind, p, reach).wait_recv()
                            for q, copy in onward:
                                if q == p:
                                    copy.start()
                            hand_on(p, kind)

    def drain():
        outgoing(lambda copy: copy.wait_send())
        crossing(lambda copy: copy.wait_send(), True, False, False)
        pair.wait_send()
        for core in range(2):
            @pl.when(h == core)
            def _(core=core):
                for s in range(ROWS):
                    forward(s, core).wait_send()
        for i in range(ROWS):
            for kind, here in enumerate((seam_left, seam_right)):
                @when(here, m == i)
                def _(i=i, kind=kind):
                    for _, copy in relays(kind, i):
                        copy.wait_send()

    pair = pltpu.make_async_remote_copy(
        src_ref=density, dst_ref=rows.at[pl.ds(ROWS * h, ROWS)],
        send_sem=pair_send, recv_sem=pair_recv,
        device_id={"wire": other}, device_id_type=MESH,
    )
    crossing(lambda copy: copy.start(), late, False, False)
    outgoing(lambda copy: copy.start())
    pair.start()

    wc_hi[...] = jnp.zeros_like(wc_hi)
    wc_lo[...] = jnp.zeros_like(wc_lo)
    place = ROWS * h + m

    def band_row(index):
        x = rows[index]
        return jnp.concatenate([x, jnp.zeros((ORB, BANDPAD - BAND), F32)], axis=1)

    def build_centre(part):
        for s in range(ROWS):
            x = band_row(ROWS * part + s)
            if s % 2:
                x = pltpu.roll(x, ORB, 1)
            high, low = split(x)
            down_by = pl.ds(pl.multiple_of(part * HALFSIDE + s * ORB, ORB), ORB)
            along = pl.ds(pl.multiple_of(part * HALFSIDE + (s - s % 2) * ORB, 128), BANDPAD)
            wc_hi[down_by, along] = high
            wc_lo[down_by, along] = low

    own.wait()
    build_centre(h)

    def framed(x):
        wide = jnp.concatenate([x, jnp.zeros((x.shape[0], FRAME - BANDPAD), F32)], axis=1)
        return pltpu.roll(wide, place * ORB, 1)

    def stack(ref, x, along):
        high, low = split(x)
        ref[0:ORB, along] = high
        ref[ORB:2 * ORB, along] = low

    stack(left, framed(band_row(place)), slice(0, FRAME))

    bits_in.wait()
    block = lax.broadcasted_iota(jnp.int32, (8, BANDPAD), 1) >> 6
    bits = jnp.zeros((8, BANDPAD), F32)
    for d in range(25):
        bits = jnp.where(block == d, pattern[m, d].astype(F32), bits)
    maskrow[...] = framed(bits)

    def product(ref, along, high, low, across):
        dims = (((1,), (1 if across else 0,)), ((), ()))
        first = lax.dot_general(ref[:, along], high, dims, preferred_element_type=F32)
        second = lax.dot_general(ref[0:ORB, along], low, dims, preferred_element_type=F32)
        return first[0:ORB] + first[ORB:2 * ORB] + second

    def centre(ref, acc):
        for b in range(9):
            a0, a1 = max(0, b - 6), min(3, b + 1)
            down_by = slice(a0 * TILE, a1 * TILE)
            along = slice(b * TILE, (b + 1) * TILE)
            acc[:, along] = product(
                ref, slice(SIDE + a0 * TILE, SIDE + a1 * TILE),
                wc_hi[down_by, along], wc_lo[down_by, along], False,
            )

    def sides(ref, acc):
        for a in range(3):
            down_by = slice(a * TILE, (a + 1) * TILE)
            lo = slice(a * TILE, SIDE)
            hi = slice(2 * SIDE, 2 * SIDE + (a + 1) * TILE)
            acc[:, SIDE + a * TILE:SIDE + (a + 1) * TILE] += (
                product(ref, lo, wc_hi[down_by, lo], wc_lo[down_by, lo], True)
                + product(ref, hi, wc_hi[down_by, hi], wc_lo[down_by, hi], True)
            )

    big_at = h * (2 * SIDE)
    small_at = 2 * SIDE - h * (2 * SIDE - HALFSIDE)

    def corners(ref, acc):
        for b in range(3):
            here = pl.ds(pl.multiple_of(big_at + b * TILE, 128), TILE)
            upto = (b + 1) * TILE
            total = product(
                ref, pl.ds(pl.multiple_of(big_at, 128), upto),
                big_hi[0:upto, b * TILE:upto], big_lo[0:upto, b * TILE:upto], False,
            )
            if b < 2:
                total += product(
                    ref, pl.ds(pl.multiple_of(big_at + upto, 128), SIDE - upto),
                    big_hi[b * TILE:upto, upto:SIDE], big_lo[b * TILE:upto, upto:SIDE], True,
                )
            acc[:, here] += total
        here = pl.ds(pl.multiple_of(small_at, 128), HALFSIDE)
        acc[:, here] += product(ref, here, small_hi[...], small_lo[...], False)

    pair.wait_recv()
    build_centre(1 - h)

    centre(left, square)
    sides(left, square)
    mid = slice(SIDE, 2 * SIDE)
    masked = square[:, mid] * maskrow[0:1, mid]
    square[:, mid] = masked
    stack(middle, masked, mid)
    centre(middle, cube)

    crossing(lambda copy: copy.start(), early, True, True)
    collect()

    def build_triangle(source_ref, high_ref, low_ref, count):
        for t in range(count):
            x = source_ref[t, :, 0:lanes(count - t)]
            if t % 2:
                x = pltpu.roll(x, ORB, 1)
                lane = lax.broadcasted_iota(jnp.int32, x.shape, 1)
                x = jnp.where(lane < ORB, 0.0, x)
            high, low = split(x)
            along = slice((t - t % 2) * ORB, count * ORB)
            high_ref[t * ORB:(t + 1) * ORB, along] = high
            low_ref[t * ORB:(t + 1) * ORB, along] = low

    build_triangle(big, big_hi, big_lo, CHIP)
    for ref in (big_hi, big_lo):
        for a in range(3):
            tile = slice(a * TILE, (a + 1) * TILE)
            ref[tile, tile] = symmetrized(ref[tile, tile])
    for s in range(ROWS):
        forward(s, 0).wait_recv()
    build_triangle(small, small_hi, small_lo, ROWS)
    for ref in (small_hi, small_lo):
        ref[...] = symmetrized(ref[...])

    corners(left, square)
    for along in (slice(0, SIDE), slice(2 * SIDE, FRAME)):
        masked = square[:, along] * maskrow[0:1, along]
        square[:, along] = masked
        stack(middle, masked, along)
    sides(middle, cube)
    corners(middle, cube)

    result = 3.0 * square[...] - 2.0 * (cube[...] * maskrow[0:1, :])
    out[0] = pltpu.roll(result, FRAME - place * ORB, 1)[:, 0:BAND]

    drain()


def on_device(density, pattern):
    dma = pltpu.SemaphoreType.DMA
    return pl.pallas_call(
        kernel,
        out_shape=jax.ShapeDtypeStruct((1, ORB, BAND), F32),
        in_specs=[pl.BlockSpec(memory_space=pltpu.HBM)] * 2,
        out_specs=pl.BlockSpec(memory_space=pltpu.VMEM),
        scratch_shapes=[
            pltpu.SMEM((ROWS, 25), jnp.int32),
            pltpu.VMEM((CHIP, ORB, BAND), F32),
            pltpu.VMEM((CHIP, ORB, SIDE), F32),
            pltpu.VMEM((ROWS, ORB, HALFSIDE), F32),
            pltpu.VMEM((SIDE, FRAME), BF16),
            pltpu.VMEM((SIDE, FRAME), BF16),
            pltpu.VMEM((SIDE, SIDE), BF16),
            pltpu.VMEM((SIDE, SIDE), BF16),
            pltpu.VMEM((HALFSIDE, HALFSIDE), BF16),
            pltpu.VMEM((HALFSIDE, HALFSIDE), BF16),
            pltpu.VMEM((2 * ORB, FRAME), BF16),
            pltpu.VMEM((2 * ORB, FRAME), BF16),
            pltpu.VMEM((ORB, FRAME), F32),
            pltpu.VMEM((ORB, FRAME), F32),
            pltpu.VMEM((8, FRAME), F32),
            dma, dma, dma, dma, dma((CHIP,)), dma((CHIP,)), dma((PIECES,)), dma((ROWS,)), dma((ROWS,)),
            dma((4, PIECES)), pltpu.SemaphoreType.REGULAR((SLOTS + 4,)),
        ],
        compiler_params=pltpu.CompilerParams(
            collective_id=0, has_side_effects=True, vmem_limit_bytes=VMEM_LIMIT
        ),
    )(density, pattern)


def solution(mesh):
    in_specs = (P("wire", None, None), P("wire", None))
    out_specs = P(("wire", "depth"), None, None)
    return jax.shard_map(
        on_device, mesh=mesh, in_specs=in_specs, out_specs=out_specs, check_vma=False
    )
```

```python
import jax
import jax.numpy as jnp
from jax import lax
from jax.experimental import pallas as pl
from jax.experimental.pallas import tpu as pltpu
from jax.sharding import PartitionSpec as P

MESH = pl.DeviceIdType.MESH
ORB = 64
ROWS = 6
CHIP = 2 * ROWS
PIECES = 3 * ROWS
FRAME = 3 * CHIP * ORB
SIDE = CHIP * ORB
HALFSIDE = ROWS * ORB
BAND = 25 * ORB
BANDPAD = 26 * ORB
TILE = 256
DIAG = 12 * ORB
F32 = jnp.float32
VMEM_LIMIT = 54000 * 1024
BF16 = jnp.bfloat16


FIRST = (8, 10, 5, 2, 1)
SECOND = (6, 7, 3, 9, 11, 4)
COMMON = (6, 8, 7, 5, 9, 10, 11)
LEFT_ORDER = (
    (8, 10, 6, 7, 9, 11, 5, 2, 3, 4, 1, 0),
    (8, 10, 5, 2, 6, 7, 3, 1, 9, 11, 4),
    (6, 7, 3, 9, 11, 4, 8, 10, 5, 2),
    (6, 7, 3, 9, 11, 4, 8, 10, 5),
    (*COMMON, 4),
    COMMON,
)
LEFT_NEXT = (
    {},
    {2: (8, 10, 5, 2), 3: (8, 10, 5), 0: (8, 10, 5, 2, 6, 7, 9, 11)},
    {1: SECOND, 3: SECOND, 4: (4,)},
    {},
    {5: COMMON},
    {},
)
RIGHT_REACH = (7, 9, 9, 10, 12, 12)
RIGHT_NEXT = ((), (0, 2), (), (), (3, 5), ())
NEXT = (LEFT_NEXT, RIGHT_NEXT)
ASIDE = {1: (8, 10), 2: (6, 7, 9, 11)}
ORDER = (
    (6, 0, 7, 8, 1, 9, 10, 11, 2, 3, 4, 5),
    (6, 0, 1, 7, 2, 8, 3, 9, 4, 10, 5, 11, 12, 13, 14, 15, 16, 17),
)
ENTRY = (
    ((5, 1, FIRST), (5, 0, (1, 3, 4, 0)), (0, 2, SECOND), (0, 4, COMMON)),
    ((5, 1, ORDER[1]), (0, 4, ORDER[1])),
)
EARLY_GIVER = (((1, 2), (1, 3), (1, 0), (2, 3), (2, 4), (4, 5)), ((1, 2), (4, 5)))
EARLY_SLOT = (2, 3, 4, 5)
SLOTS = 6
LAST_SLOT = 1


def row_of(p):
    return p % CHIP


def core_of(p):
    return row_of(p) // ROWS


def cores_of(order):
    return sorted({core_of(p) for p in order})


def lanes(blocks):
    return (blocks + 1) // 2 * 2 * ORB


def split(x):
    high = x.astype(BF16)
    low = (x - high.astype(F32)).astype(BF16)
    return high, low


def symmetrized(tile):
    size = tile.shape[0]
    row = lax.broadcasted_iota(jnp.int32, (size, size), 0) >> 6
    col = lax.broadcasted_iota(jnp.int32, (size, size), 1) >> 6
    tile = tile.astype(F32)
    return jnp.where(row <= col, tile, tile.T).astype(BF16)


def kernel(
    density, pattern_in, out,
    pattern, rows, big, small, wc_hi, wc_lo, big_hi, big_lo, small_hi, small_lo,
    left, middle, square, cube, maskrow,
    pattern_sem, own_sem, pair_send, pair_recv, up_send, down_send, big_recv, fwd_send, fwd_recv, relay_send, ready,
):
    wire = lax.axis_index("wire")
    length = lax.axis_size("wire")
    me = lax.axis_index("depth")
    m = me
    half = length // 4
    spot = lax.rem(wire // 2, half)
    h = lax.rem(wire, 2)
    other = wire + 1 - 2 * h
    up = lax.rem(wire - h + 2, length)
    down = lax.rem(wire - h - 1 + length, length)
    source = lax.rem(wire - h + 4 * h - 2 + length, length)

    own = pltpu.make_async_copy(density, rows.at[pl.ds(ROWS * h, ROWS)], own_sem)
    own.start()
    bits_in = pltpu.make_async_copy(pattern_in, pattern, pattern_sem)
    bits_in.start()

    first = spot == 0
    last = spot == half - 1
    seam_left = jnp.logical_and(h == 0, first)
    seam_right = jnp.logical_and(h == 1, last)
    seam = jnp.logical_or(seam_left, seam_right)
    ends = jnp.logical_or(m == 0, m == 5)
    late = 2 * wire >= length
    early = jnp.logical_not(late)
    barrier = pltpu.get_barrier_semaphore()

    def greet(w, d):
        pl.semaphore_signal(barrier, inc=1, device_id={"wire": w, "depth": d}, device_id_type=MESH)

    def when(cond, *more):
        for c in more:
            if c is not True:
                cond = jnp.logical_and(cond, c)
        return pl.when(cond)

    @pl.when(seam)
    def _():
        big[...] = jnp.zeros_like(big)

    greet(other, me)
    expected = jnp.int32(1)

    def counted(cond, n):
        return jnp.where(cond, n, 0)

    @pl.when(jnp.logical_not(seam))
    def _():
        greet(source, me)
        greet(source + 1, me)

    expected += counted(jnp.logical_not(first), 1) + counted(jnp.logical_not(last), 1)
    entries = [
        (slot, kind, (last, first)[kind], (up, down)[kind], (seam_left, seam_right)[kind], *entry)
        for slot, (kind, entry) in enumerate((k, e) for k in range(2) for e in ENTRY[k])
    ]
    for slot, kind, end, target, here, giver, taker, order in entries:
        for core in cores_of(order):
            gives = jnp.logical_and(jnp.logical_and(end, h == core), m == giver)
            takes = jnp.logical_and(here, m == taker)
            if slot in EARLY_SLOT:
                expected += counted(jnp.logical_and(gives, late), 1)
                expected += counted(jnp.logical_and(takes, late), 1)

                @when(gives, early)
                def _(target=target, taker=taker):
                    greet(target, taker)
            else:
                expected += counted(gives, 1)

            @when(takes, early if slot in EARLY_SLOT else True)
            def _(giver=giver, core=core):
                greet(source + core, giver)

    for kind, here in enumerate((seam_left, seam_right)):
        for giver in range(ROWS):
            for taker in NEXT[kind][giver]:
                asks = (giver, taker) in EARLY_GIVER[kind]
                @when(here, m == (giver if asks else taker))
                def _(peer=taker if asks else giver):
                    greet(wire, peer)
                expected += counted(
                    jnp.logical_and(here, m == (taker if asks else giver)), 1
                )
    beside = jnp.logical_and(jnp.logical_and(h == 1, first), m == 0)
    served = jnp.logical_and(seam_left, m == 0)
    for giver in ASIDE:
        expected += counted(jnp.logical_and(seam_left, m == giver), 1)

        @pl.when(beside)
        def _(giver=giver):
            greet(other, giver)

    pl.semaphore_wait(barrier, expected)

    def is_ready(w, d, slot):
        pl.semaphore_signal(
            ready.at[slot], inc=1, device_id={"wire": w, "depth": d}, device_id_type=MESH
        )

    for slot, kind, end, target, here, giver, taker, order in entries:
        for core in cores_of(order) if slot in EARLY_SLOT else ():
            @when(here, late, m == taker)
            def _(giver=giver, core=core, slot=slot):
                is_ready(source + core, giver, slot)

    for kind, here in enumerate((seam_left, seam_right)):
        for giver in range(ROWS):
            for n, taker in enumerate(NEXT[kind][giver]):
                if (giver, taker) in EARLY_GIVER[kind]:
                    @when(here, m == taker)
                    def _(giver=giver, n=n):
                        is_ready(wire, giver, SLOTS + n)

    def part(kind, p, reach):
        t = row_of(p)
        if kind == 0 or t >= ROWS:
            return t, 0, lanes(reach - t)
        near = lanes(ROWS - t)
        return (t, 0, near) if p < CHIP else (t, near, lanes(reach - t) - near)

    def row_copy(kind, p, reach, target, depth, second=0):
        t, start, width = part(kind, p, reach)
        sem = down_send.at[t % ROWS + p // CHIP * ROWS] if kind else up_send.at[t % ROWS + second * ROWS]
        return pltpu.make_async_remote_copy(
            src_ref=density.at[t % ROWS, :, pl.ds(DIAG + start, width)],
            dst_ref=big.at[t, :, pl.ds(start, width)],
            send_sem=sem, recv_sem=big_recv.at[p],
            device_id={"wire": target, "depth": depth}, device_id_type=MESH,
        )

    def present(kind, p, reach):
        return row_of(p) < reach and part(kind, p, reach)[2] > 0

    def send(act, kind, core, order, target, depth, reach, second=0):
        for p in order:
            if core_of(p) == core and present(kind, p, reach):
                act(row_copy(kind, p, reach, target, depth, second))

    def outgoing(act):
        for core in range(2):
            @when(h == core, jnp.logical_not(first))
            def _(core=core):
                send(act, 1, core, ORDER[1][:CHIP], down, me, CHIP)

            @when(h == core, jnp.logical_not(last))
            def _(core=core):
                send(act, 0, core, ORDER[0], up, me, CHIP)

            @when(h == core, jnp.logical_not(first))
            def _(core=core):
                send(act, 1, core, ORDER[1][CHIP:], down, me, CHIP)

    def crossing(act, stage):
        for slot, kind, end, target, here, giver, taker, order in entries:
            answered = slot in EARLY_SLOT and stage == 1
            if stage < 2 and slot not in EARLY_SLOT and (slot == LAST_SLOT) != (stage == 1):
                continue
            whose = (late, early, True)[stage] if slot in EARLY_SLOT else True
            for core in cores_of(order):
                @when(h == core, whose, end, m == giver)
                def _(core=core, slot=slot, kind=kind, target=target, taker=taker, order=order, answered=answered):
                    if answered:
                        pl.semaphore_wait(ready.at[slot], 1)
                    reach = RIGHT_REACH[taker] if kind else CHIP
                    send(act, kind, core, order, target, taker, reach, slot in (1, 3))

    def arriving(kind, p, reach):
        return row_copy(kind, p, reach, up, me)

    def relay(kind, p, reach, depth, n):
        t, start, width = part(kind, p, reach)
        return pltpu.make_async_remote_copy(
            src_ref=big.at[t, :, pl.ds(start, width)],
            dst_ref=big.at[t, :, pl.ds(start, width)],
            send_sem=relay_send.at[n, p], recv_sem=big_recv.at[p],
            device_id={"wire": wire, "depth": depth}, device_id_type=MESH,
        )

    def forward(s, core):
        width = lanes(ROWS - s)
        return pltpu.make_async_remote_copy(
            src_ref=big.at[ROWS * (1 - core) + s, :, pl.ds(0, width)],
            dst_ref=small.at[s, :, pl.ds(0, width)],
            send_sem=fwd_send.at[s], recv_sem=fwd_recv.at[s],
            device_id={"wire": other}, device_id_type=MESH,
        )

    def aside(t, n):
        width = lanes(CHIP - t)
        return pltpu.make_async_remote_copy(
            src_ref=big.at[t, :, pl.ds(0, width)],
            dst_ref=small.at[t - ROWS, :, pl.ds(0, width)],
            send_sem=relay_send.at[n, t], recv_sem=fwd_recv.at[t - ROWS],
            device_id={"wire": other, "depth": 0}, device_id_type=MESH,
        )

    def hand_on(p, core):
        if p < CHIP and core_of(p) == 1 - core:
            forward(p % ROWS, core).start()

    def relays(kind, i):
        if kind == 0:
            for p in ASIDE.get(i, ()):
                yield p, aside(p, 4)
            for n, (target, which) in enumerate(LEFT_NEXT[i].items()):
                for p in LEFT_ORDER[i]:
                    if p in which and p in LEFT_ORDER[target]:
                        yield p, relay(0, p, CHIP, target, n)
        for n, target in enumerate(RIGHT_NEXT[i] if kind else ()):
            for p in ORDER[1]:
                if present(1, p, RIGHT_REACH[target]):
                    yield p, relay(1, p, RIGHT_REACH[target], target, n)

    def collect():
        for core in range(2):
            @when(h == core, jnp.logical_not(seam))
            def _(core=core):
                for near in (True, False):
                    for p in ORDER[core]:
                        if (p < CHIP and core_of(p) == 1 - core) == near:
                            arriving(core, p, CHIP).wait_recv()
                            hand_on(p, core)
        for i in range(ROWS):
            for kind, here in enumerate((seam_left, seam_right)):
                @when(here, m == i)
                def _(i=i, kind=kind):
                    order = ORDER[1] if kind else LEFT_ORDER[i]
                    reach = RIGHT_REACH[i] if kind else CHIP
                    onward = list(relays(kind, i))
                    for n, taker in enumerate(NEXT[kind][i]):
                        if (i, taker) in EARLY_GIVER[kind]:
                            pl.semaphore_wait(ready.at[SLOTS + n], 1)
                    for p in order:
                        if present(kind, p, reach):
                            arriving(kind, p, reach).wait_recv()
                            for q, copy in onward:
                                if q == p:
                                    copy.start()
                            if kind or i:
                                hand_on(p, kind)

    def drain():
        outgoing(lambda copy: copy.wait_send())
        crossing(lambda copy: copy.wait_send(), 2)
        pair.wait_send()
        for core in range(2):
            @when(h == core, jnp.logical_not(served))
            def _(core=core):
                for s in range(ROWS):
                    forward(s, core).wait_send()
        for i in range(ROWS):
            for kind, here in enumerate((seam_left, seam_right)):
                @when(here, m == i)
                def _(i=i, kind=kind):
                    for _, copy in relays(kind, i):
                        copy.wait_send()

    pair = pltpu.make_async_remote_copy(
        src_ref=density, dst_ref=rows.at[pl.ds(ROWS * h, ROWS)],
        send_sem=pair_send, recv_sem=pair_recv,
        device_id={"wire": other}, device_id_type=MESH,
    )
    crossing(lambda copy: copy.start(), 0)
    outgoing(lambda copy: copy.start())
    pair.start()

    wc_hi[...] = jnp.zeros_like(wc_hi)
    wc_lo[...] = jnp.zeros_like(wc_lo)
    place = ROWS * h + m

    def band_row(index):
        x = rows[index]
        return jnp.concatenate([x, jnp.zeros((ORB, BANDPAD - BAND), F32)], axis=1)

    def build_centre(part):
        for s in range(ROWS):
            x = band_row(ROWS * part + s)
            if s % 2:
                x = pltpu.roll(x, ORB, 1)
            high, low = split(x)
            down_by = pl.ds(pl.multiple_of(part * HALFSIDE + s * ORB, ORB), ORB)
            along = pl.ds(pl.multiple_of(part * HALFSIDE + (s - s % 2) * ORB, 128), BANDPAD)
            wc_hi[down_by, along] = high
            wc_lo[down_by, along] = low

    own.wait()
    build_centre(h)

    def framed(x):
        wide = jnp.concatenate([x, jnp.zeros((x.shape[0], FRAME - BANDPAD), F32)], axis=1)
        return pltpu.roll(wide, place * ORB, 1)

    def stack(ref, x, along):
        high, low = split(x)
        ref[0:ORB, along] = high
        ref[ORB:2 * ORB, along] = low

    stack(left, framed(band_row(place)), slice(0, FRAME))

    bits_in.wait()
    block = lax.broadcasted_iota(jnp.int32, (8, BANDPAD), 1) >> 6
    bits = jnp.zeros((8, BANDPAD), F32)
    for d in range(25):
        bits = jnp.where(block == d, pattern[m, d].astype(F32), bits)
    maskrow[...] = framed(bits)

    def product(ref, along, high, low, across):
        dims = (((1,), (1 if across else 0,)), ((), ()))
        first = lax.dot_general(ref[:, along], high, dims, preferred_element_type=F32)
        second = lax.dot_general(ref[0:ORB, along], low, dims, preferred_element_type=F32)
        return first[0:ORB] + first[ORB:2 * ORB] + second

    def centre(ref, acc):
        for b in range(9):
            a0, a1 = max(0, b - 6), min(3, b + 1)
            down_by = slice(a0 * TILE, a1 * TILE)
            along = slice(b * TILE, (b + 1) * TILE)
            acc[:, along] = product(
                ref, slice(SIDE + a0 * TILE, SIDE + a1 * TILE),
                wc_hi[down_by, along], wc_lo[down_by, along], False,
            )

    def sides(ref, acc):
        for a in range(3):
            down_by = slice(a * TILE, (a + 1) * TILE)
            lo = slice(a * TILE, SIDE)
            hi = slice(2 * SIDE, 2 * SIDE + (a + 1) * TILE)
            acc[:, SIDE + a * TILE:SIDE + (a + 1) * TILE] += (
                product(ref, lo, wc_hi[down_by, lo], wc_lo[down_by, lo], True)
                + product(ref, hi, wc_hi[down_by, hi], wc_lo[down_by, hi], True)
            )

    big_at = h * (2 * SIDE)
    small_at = 2 * SIDE - h * (2 * SIDE - HALFSIDE)

    def corners(ref, acc):
        for b in range(3):
            here = pl.ds(pl.multiple_of(big_at + b * TILE, 128), TILE)
            upto = (b + 1) * TILE
            total = product(
                ref, pl.ds(pl.multiple_of(big_at, 128), upto),
                big_hi[0:upto, b * TILE:upto], big_lo[0:upto, b * TILE:upto], False,
            )
            if b < 2:
                total += product(
                    ref, pl.ds(pl.multiple_of(big_at + upto, 128), SIDE - upto),
                    big_hi[b * TILE:upto, upto:SIDE], big_lo[b * TILE:upto, upto:SIDE], True,
                )
            acc[:, here] += total
        here = pl.ds(pl.multiple_of(small_at, 128), HALFSIDE)
        acc[:, here] += product(ref, here, small_hi[...], small_lo[...], False)

    pair.wait_recv()
    build_centre(1 - h)

    centre(left, square)
    sides(left, square)
    mid = slice(SIDE, 2 * SIDE)
    masked = square[:, mid] * maskrow[0:1, mid]
    square[:, mid] = masked
    stack(middle, masked, mid)
    centre(middle, cube)

    crossing(lambda copy: copy.start(), 1)
    collect()

    def build_triangle(source_ref, high_ref, low_ref, count):
        for t in range(count):
            x = source_ref[t, :, 0:lanes(count - t)]
            if t % 2:
                x = pltpu.roll(x, ORB, 1)
                lane = lax.broadcasted_iota(jnp.int32, x.shape, 1)
                x = jnp.where(lane < ORB, 0.0, x)
            high, low = split(x)
            along = slice((t - t % 2) * ORB, count * ORB)
            high_ref[t * ORB:(t + 1) * ORB, along] = high
            low_ref[t * ORB:(t + 1) * ORB, along] = low

    build_triangle(big, big_hi, big_lo, CHIP)
    for ref in (big_hi, big_lo):
        for a in range(3):
            tile = slice(a * TILE, (a + 1) * TILE)
            ref[tile, tile] = symmetrized(ref[tile, tile])
    for s in range(ROWS):
        forward(s, 0).wait_recv()
    build_triangle(small, small_hi, small_lo, ROWS)
    for ref in (small_hi, small_lo):
        ref[...] = symmetrized(ref[...])

    corners(left, square)
    for along in (slice(0, SIDE), slice(2 * SIDE, FRAME)):
        masked = square[:, along] * maskrow[0:1, along]
        square[:, along] = masked
        stack(middle, masked, along)
    sides(middle, cube)
    corners(middle, cube)

    result = 3.0 * square[...] - 2.0 * (cube[...] * maskrow[0:1, :])
    out[0] = pltpu.roll(result, FRAME - place * ORB, 1)[:, 0:BAND]

    drain()


def on_device(density, pattern):
    dma = pltpu.SemaphoreType.DMA
    return pl.pallas_call(
        kernel,
        out_shape=jax.ShapeDtypeStruct((1, ORB, BAND), F32),
        in_specs=[pl.BlockSpec(memory_space=pltpu.HBM)] * 2,
        out_specs=pl.BlockSpec(memory_space=pltpu.VMEM),
        scratch_shapes=[
            pltpu.SMEM((ROWS, 25), jnp.int32),
            pltpu.VMEM((CHIP, ORB, BAND), F32),
            pltpu.VMEM((CHIP, ORB, SIDE), F32),
            pltpu.VMEM((ROWS, ORB, HALFSIDE), F32),
            pltpu.VMEM((SIDE, FRAME), BF16),
            pltpu.VMEM((SIDE, FRAME), BF16),
            pltpu.VMEM((SIDE, SIDE), BF16),
            pltpu.VMEM((SIDE, SIDE), BF16),
            pltpu.VMEM((HALFSIDE, HALFSIDE), BF16),
            pltpu.VMEM((HALFSIDE, HALFSIDE), BF16),
            pltpu.VMEM((2 * ORB, FRAME), BF16),
            pltpu.VMEM((2 * ORB, FRAME), BF16),
            pltpu.VMEM((ORB, FRAME), F32),
            pltpu.VMEM((ORB, FRAME), F32),
            pltpu.VMEM((8, FRAME), F32),
            dma, dma, dma, dma, dma((CHIP,)), dma((CHIP,)), dma((PIECES,)), dma((ROWS,)), dma((ROWS,)),
            dma((5, PIECES)), pltpu.SemaphoreType.REGULAR((SLOTS + 4,)),
        ],
        compiler_params=pltpu.CompilerParams(
            collective_id=0, has_side_effects=True, vmem_limit_bytes=VMEM_LIMIT
        ),
    )(density, pattern)


def solution(mesh):
    in_specs = (P("wire", None, None), P("wire", None))
    out_specs = P(("wire", "depth"), None, None)
    return jax.shard_map(
        on_device, mesh=mesh, in_specs=in_specs, out_specs=out_specs, check_vma=False
    )
```

```python
import jax
import jax.numpy as jnp
from jax import lax
from jax.experimental import pallas as pl
from jax.experimental.pallas import tpu as pltpu
from jax.sharding import PartitionSpec as P

MESH = pl.DeviceIdType.MESH
ORB = 64
ROWS = 6
CHIP = 2 * ROWS
PIECES = 3 * ROWS
FRAME = 3 * CHIP * ORB
SIDE = CHIP * ORB
HALFSIDE = ROWS * ORB
BAND = 25 * ORB
BANDPAD = 26 * ORB
TILE = 256
DIAG = 12 * ORB
F32 = jnp.float32
VMEM_LIMIT = 54000 * 1024
BF16 = jnp.bfloat16


FIRST = (8, 10, 5, 2, 1)
SECOND = (6, 7, 3, 9, 11, 4)
COMMON = (6, 8, 7, 5, 9, 10, 11)
LEFT_ORDER = (
    (8, 10, 6, 7, 9, 11, 5, 2, 3, 4, 1, 0),
    (8, 10, 5, 2, 6, 7, 3, 1, 9, 11, 4),
    (6, 7, 3, 9, 11, 4, 8, 10, 5, 2),
    (6, 7, 3, 9, 11, 4, 8, 10, 5),
    (*COMMON, 4),
    COMMON,
)
LEFT_NEXT = (
    {},
    {2: (8, 10, 5, 2), 3: (8, 10, 5), 0: (8, 10, 5, 2, 6, 7, 9, 11)},
    {1: (6, 7, 3, 9, 11), 3: SECOND, 4: (4,)},
    {},
    {5: COMMON},
    {},
)
RIGHT_REACH = (7, 9, 9, 10, 12, 12)
RIGHT_NEXT = ((), (0, 2), (), (), (3, 5), ())
NEXT = (LEFT_NEXT, RIGHT_NEXT)
ASIDE = {1: (8, 10), 2: (6, 7, 9, 11)}
ORDER = (
    (6, 0, 7, 8, 1, 9, 10, 11, 2, 3, 4, 5),
    (6, 0, 1, 7, 2, 8, 3, 9, 4, 10, 5, 11, 12, 13, 14, 15, 16, 17),
)
ENTRY = (
    ((5, 1, FIRST), (5, 0, (1, 3, 4, 0)), (0, 2, SECOND), (0, 1, (4,)), (0, 4, COMMON)),
    ((5, 1, ORDER[1]), (0, 4, ORDER[1])),
)
EARLY_GIVER = (((1, 2), (1, 3), (1, 0), (2, 3), (2, 4), (4, 5)), ((1, 2), (4, 5)))
EARLY_SLOT = (2, 3, 4, 5, 6)
SLOTS = 7
LAST_SLOT = 1


def row_of(p):
    return p % CHIP


def core_of(p):
    return row_of(p) // ROWS


def cores_of(order):
    return sorted({core_of(p) for p in order})


def lanes(blocks):
    return (blocks + 1) // 2 * 2 * ORB


def split(x):
    high = x.astype(BF16)
    low = (x - high.astype(F32)).astype(BF16)
    return high, low


def symmetrized(tile):
    size = tile.shape[0]
    row = lax.broadcasted_iota(jnp.int32, (size, size), 0) >> 6
    col = lax.broadcasted_iota(jnp.int32, (size, size), 1) >> 6
    tile = tile.astype(F32)
    return jnp.where(row <= col, tile, tile.T).astype(BF16)


def kernel(
    density, pattern_in, out,
    pattern, rows, big, small, wc_hi, wc_lo, big_hi, big_lo, small_hi, small_lo,
    left, middle, square, cube, maskrow,
    pattern_sem, own_sem, pair_send, pair_recv, up_send, down_send, big_recv, fwd_send, fwd_recv, relay_send, ready,
):
    wire = lax.axis_index("wire")
    length = lax.axis_size("wire")
    me = lax.axis_index("depth")
    m = me
    half = length // 4
    spot = lax.rem(wire // 2, half)
    h = lax.rem(wire, 2)
    other = wire + 1 - 2 * h
    up = lax.rem(wire - h + 2, length)
    down = lax.rem(wire - h - 1 + length, length)
    source = lax.rem(wire - h + 4 * h - 2 + length, length)

    own = pltpu.make_async_copy(density, rows.at[pl.ds(ROWS * h, ROWS)], own_sem)
    own.start()
    bits_in = pltpu.make_async_copy(pattern_in, pattern, pattern_sem)
    bits_in.start()

    first = spot == 0
    last = spot == half - 1
    seam_left = jnp.logical_and(h == 0, first)
    seam_right = jnp.logical_and(h == 1, last)
    seam = jnp.logical_or(seam_left, seam_right)
    ends = jnp.logical_or(m == 0, m == 5)
    late = 2 * wire >= length
    early = jnp.logical_not(late)
    barrier = pltpu.get_barrier_semaphore()

    def greet(w, d):
        pl.semaphore_signal(barrier, inc=1, device_id={"wire": w, "depth": d}, device_id_type=MESH)

    def when(cond, *more):
        for c in more:
            if c is not True:
                cond = jnp.logical_and(cond, c)
        return pl.when(cond)

    greet(other, me)

    @pl.when(seam)
    def _():
        big[...] = jnp.zeros_like(big)

    expected = jnp.int32(1)

    def counted(cond, n):
        return jnp.where(cond, n, 0)

    @pl.when(jnp.logical_not(seam))
    def _():
        greet(source, me)
        greet(source + 1, me)

    expected += counted(jnp.logical_not(first), 1) + counted(jnp.logical_not(last), 1)
    entries = [
        (slot, kind, (last, first)[kind], (up, down)[kind], (seam_left, seam_right)[kind], *entry)
        for slot, (kind, entry) in enumerate((k, e) for k in range(2) for e in ENTRY[k])
    ]
    for slot, kind, end, target, here, giver, taker, order in entries:
        for core in cores_of(order):
            gives = jnp.logical_and(jnp.logical_and(end, h == core), m == giver)
            takes = jnp.logical_and(here, m == taker)
            if slot in EARLY_SLOT:
                expected += counted(jnp.logical_and(gives, late), 1)
                expected += counted(jnp.logical_and(takes, late), 1)

                @when(gives, early)
                def _(target=target, taker=taker):
                    greet(target, taker)
            else:
                expected += counted(gives, 1)

            @when(takes, early if slot in EARLY_SLOT else True)
            def _(giver=giver, core=core):
                greet(source + core, giver)

    for kind, here in enumerate((seam_left, seam_right)):
        for giver in range(ROWS):
            for taker in NEXT[kind][giver]:
                asks = (giver, taker) in EARLY_GIVER[kind]
                @when(here, m == (giver if asks else taker))
                def _(peer=taker if asks else giver):
                    greet(wire, peer)
                expected += counted(
                    jnp.logical_and(here, m == (taker if asks else giver)), 1
                )
    beside = jnp.logical_and(jnp.logical_and(h == 1, first), m == 0)
    served = jnp.logical_and(seam_left, m == 0)
    for giver in ASIDE:
        expected += counted(jnp.logical_and(seam_left, m == giver), 1)

        @pl.when(beside)
        def _(giver=giver):
            greet(other, giver)

    pl.semaphore_wait(barrier, expected)

    def is_ready(w, d, slot):
        pl.semaphore_signal(
            ready.at[slot], inc=1, device_id={"wire": w, "depth": d}, device_id_type=MESH
        )

    for slot, kind, end, target, here, giver, taker, order in entries:
        for core in cores_of(order) if slot in EARLY_SLOT else ():
            @when(here, late, m == taker)
            def _(giver=giver, core=core, slot=slot):
                is_ready(source + core, giver, slot)

    for kind, here in enumerate((seam_left, seam_right)):
        for giver in range(ROWS):
            for n, taker in enumerate(NEXT[kind][giver]):
                if (giver, taker) in EARLY_GIVER[kind]:
                    @when(here, m == taker)
                    def _(giver=giver, n=n):
                        is_ready(wire, giver, SLOTS + n)

    def part(kind, p, reach):
        t = row_of(p)
        if kind == 0 or t >= ROWS:
            return t, 0, lanes(reach - t)
        near = lanes(ROWS - t)
        return (t, 0, near) if p < CHIP else (t, near, lanes(reach - t) - near)

    def row_copy(kind, p, reach, target, depth, second=0):
        t, start, width = part(kind, p, reach)
        sem = down_send.at[t % ROWS + p // CHIP * ROWS] if kind else up_send.at[t % ROWS + second * ROWS]
        return pltpu.make_async_remote_copy(
            src_ref=density.at[t % ROWS, :, pl.ds(DIAG + start, width)],
            dst_ref=big.at[t, :, pl.ds(start, width)],
            send_sem=sem, recv_sem=big_recv.at[p],
            device_id={"wire": target, "depth": depth}, device_id_type=MESH,
        )

    def present(kind, p, reach):
        return row_of(p) < reach and part(kind, p, reach)[2] > 0

    def send(act, kind, core, order, target, depth, reach, second=0):
        for p in order:
            if core_of(p) == core and present(kind, p, reach):
                act(row_copy(kind, p, reach, target, depth, second))

    def outgoing(act):
        for core in range(2):
            @when(h == core, jnp.logical_not(first))
            def _(core=core):
                send(act, 1, core, ORDER[1][:CHIP], down, me, CHIP)

            @when(h == core, jnp.logical_not(last))
            def _(core=core):
                send(act, 0, core, ORDER[0], up, me, CHIP)

            @when(h == core, jnp.logical_not(first))
            def _(core=core):
                send(act, 1, core, ORDER[1][CHIP:], down, me, CHIP)

    def crossing(act, stage):
        for slot, kind, end, target, here, giver, taker, order in entries:
            answered = slot in EARLY_SLOT and stage == 1
            if stage < 2 and slot not in EARLY_SLOT and (slot == LAST_SLOT) != (stage == 1):
                continue
            whose = (late, early, True)[stage] if slot in EARLY_SLOT else True
            for core in cores_of(order):
                @when(h == core, whose, end, m == giver)
                def _(core=core, slot=slot, kind=kind, target=target, taker=taker, order=order, answered=answered):
                    if answered:
                        pl.semaphore_wait(ready.at[slot], 1)
                    reach = RIGHT_REACH[taker] if kind else CHIP
                    send(act, kind, core, order, target, taker, reach, slot in (1, 3, 4))

    def arriving(kind, p, reach):
        return row_copy(kind, p, reach, up, me)

    def relay(kind, p, reach, depth, n):
        t, start, width = part(kind, p, reach)
        return pltpu.make_async_remote_copy(
            src_ref=big.at[t, :, pl.ds(start, width)],
            dst_ref=big.at[t, :, pl.ds(start, width)],
            send_sem=relay_send.at[n, p], recv_sem=big_recv.at[p],
            device_id={"wire": wire, "depth": depth}, device_id_type=MESH,
        )

    def forward(s, core):
        width = lanes(ROWS - s)
        return pltpu.make_async_remote_copy(
            src_ref=big.at[ROWS * (1 - core) + s, :, pl.ds(0, width)],
            dst_ref=small.at[s, :, pl.ds(0, width)],
            send_sem=fwd_send.at[s], recv_sem=fwd_recv.at[s],
            device_id={"wire": other}, device_id_type=MESH,
        )

    def aside(t, n):
        width = lanes(CHIP - t)
        return pltpu.make_async_remote_copy(
            src_ref=big.at[t, :, pl.ds(0, width)],
            dst_ref=small.at[t - ROWS, :, pl.ds(0, width)],
            send_sem=relay_send.at[n, t], recv_sem=fwd_recv.at[t - ROWS],
            device_id={"wire": other, "depth": 0}, device_id_type=MESH,
        )

    def hand_on(p, core):
        if p < CHIP and core_of(p) == 1 - core:
            forward(p % ROWS, core).start()

    def relays(kind, i):
        if kind == 0:
            for p in ASIDE.get(i, ()):
                yield p, aside(p, 4)
            for n, (target, which) in enumerate(LEFT_NEXT[i].items()):
                for p in LEFT_ORDER[i]:
                    if p in which and p in LEFT_ORDER[target]:
                        yield p, relay(0, p, CHIP, target, n)
        for n, target in enumerate(RIGHT_NEXT[i] if kind else ()):
            for p in ORDER[1]:
                if present(1, p, RIGHT_REACH[target]):
                    yield p, relay(1, p, RIGHT_REACH[target], target, n)

    def collect():
        for core in range(2):
            @when(h == core, jnp.logical_not(seam))
            def _(core=core):
                for near in (True, False):
                    for p in ORDER[core]:
                        if (p < CHIP and core_of(p) == 1 - core) == near:
                            arriving(core, p, CHIP).wait_recv()
                            hand_on(p, core)
        for i in range(ROWS):
            for kind, here in enumerate((seam_left, seam_right)):
                @when(here, m == i)
                def _(i=i, kind=kind):
                    order = ORDER[1] if kind else LEFT_ORDER[i]
                    reach = RIGHT_REACH[i] if kind else CHIP
                    onward = list(relays(kind, i))
                    for n, taker in enumerate(NEXT[kind][i]):
                        if (i, taker) in EARLY_GIVER[kind]:
                            pl.semaphore_wait(ready.at[SLOTS + n], 1)
                    for p in order:
                        if present(kind, p, reach):
                            arriving(kind, p, reach).wait_recv()
                            for q, copy in onward:
                                if q == p:
                                    copy.start()
                            if kind or i:
                                hand_on(p, kind)

    def drain():
        outgoing(lambda copy: copy.wait_send())
        crossing(lambda copy: copy.wait_send(), 2)
        pair.wait_send()
        for core in range(2):
            @when(h == core, jnp.logical_not(served))
            def _(core=core):
                for s in range(ROWS):
                    forward(s, core).wait_send()
        for i in range(ROWS):
            for kind, here in enumerate((seam_left, seam_right)):
                @when(here, m == i)
                def _(i=i, kind=kind):
                    for _, copy in relays(kind, i):
                        copy.wait_send()

    pair = pltpu.make_async_remote_copy(
        src_ref=density, dst_ref=rows.at[pl.ds(ROWS * h, ROWS)],
        send_sem=pair_send, recv_sem=pair_recv,
        device_id={"wire": other}, device_id_type=MESH,
    )
    crossing(lambda copy: copy.start(), 0)
    outgoing(lambda copy: copy.start())
    pair.start()

    wc_hi[...] = jnp.zeros_like(wc_hi)
    wc_lo[...] = jnp.zeros_like(wc_lo)
    place = ROWS * h + m

    def band_row(index):
        x = rows[index]
        return jnp.concatenate([x, jnp.zeros((ORB, BANDPAD - BAND), F32)], axis=1)

    def build_centre(part):
        for s in range(ROWS):
            x = band_row(ROWS * part + s)
            if s % 2:
                x = pltpu.roll(x, ORB, 1)
            high, low = split(x)
            down_by = pl.ds(pl.multiple_of(part * HALFSIDE + s * ORB, ORB), ORB)
            along = pl.ds(pl.multiple_of(part * HALFSIDE + (s - s % 2) * ORB, 128), BANDPAD)
            wc_hi[down_by, along] = high
            wc_lo[down_by, along] = low

    own.wait()
    build_centre(h)

    def framed(x):
        wide = jnp.concatenate([x, jnp.zeros((x.shape[0], FRAME - BANDPAD), F32)], axis=1)
        return pltpu.roll(wide, place * ORB, 1)

    def stack(ref, x, along):
        high, low = split(x)
        ref[0:ORB, along] = high
        ref[ORB:2 * ORB, along] = low

    stack(left, framed(band_row(place)), slice(0, FRAME))

    bits_in.wait()
    block = lax.broadcasted_iota(jnp.int32, (8, BANDPAD), 1) >> 6
    bits = jnp.zeros((8, BANDPAD), F32)
    for d in range(25):
        bits = jnp.where(block == d, pattern[m, d].astype(F32), bits)
    maskrow[...] = framed(bits)

    def product(ref, along, high, low, across):
        dims = (((1,), (1 if across else 0,)), ((), ()))
        first = lax.dot_general(ref[:, along], high, dims, preferred_element_type=F32)
        second = lax.dot_general(ref[0:ORB, along], low, dims, preferred_element_type=F32)
        return first[0:ORB] + first[ORB:2 * ORB] + second

    def centre(ref, acc):
        for b in range(9):
            a0, a1 = max(0, b - 6), min(3, b + 1)
            down_by = slice(a0 * TILE, a1 * TILE)
            along = slice(b * TILE, (b + 1) * TILE)
            acc[:, along] = product(
                ref, slice(SIDE + a0 * TILE, SIDE + a1 * TILE),
                wc_hi[down_by, along], wc_lo[down_by, along], False,
            )

    def sides(ref, acc):
        for a in range(3):
            down_by = slice(a * TILE, (a + 1) * TILE)
            lo = slice(a * TILE, SIDE)
            hi = slice(2 * SIDE, 2 * SIDE + (a + 1) * TILE)
            acc[:, SIDE + a * TILE:SIDE + (a + 1) * TILE] += (
                product(ref, lo, wc_hi[down_by, lo], wc_lo[down_by, lo], True)
                + product(ref, hi, wc_hi[down_by, hi], wc_lo[down_by, hi], True)
            )

    big_at = h * (2 * SIDE)
    small_at = 2 * SIDE - h * (2 * SIDE - HALFSIDE)

    def corners(ref, acc):
        for b in range(3):
            here = pl.ds(pl.multiple_of(big_at + b * TILE, 128), TILE)
            upto = (b + 1) * TILE
            total = product(
                ref, pl.ds(pl.multiple_of(big_at, 128), upto),
                big_hi[0:upto, b * TILE:upto], big_lo[0:upto, b * TILE:upto], False,
            )
            if b < 2:
                total += product(
                    ref, pl.ds(pl.multiple_of(big_at + upto, 128), SIDE - upto),
                    big_hi[b * TILE:upto, upto:SIDE], big_lo[b * TILE:upto, upto:SIDE], True,
                )
            acc[:, here] += total
        here = pl.ds(pl.multiple_of(small_at, 128), HALFSIDE)
        acc[:, here] += product(ref, here, small_hi[...], small_lo[...], False)

    pair.wait_recv()
    build_centre(1 - h)

    centre(left, square)
    sides(left, square)
    mid = slice(SIDE, 2 * SIDE)
    masked = square[:, mid] * maskrow[0:1, mid]
    square[:, mid] = masked
    stack(middle, masked, mid)
    centre(middle, cube)

    crossing(lambda copy: copy.start(), 1)
    collect()

    def build_triangle(source_ref, high_ref, low_ref, count):
        for t in range(count):
            x = source_ref[t, :, 0:lanes(count - t)]
            if t % 2:
                x = pltpu.roll(x, ORB, 1)
                lane = lax.broadcasted_iota(jnp.int32, x.shape, 1)
                x = jnp.where(lane < ORB, 0.0, x)
            high, low = split(x)
            along = slice((t - t % 2) * ORB, count * ORB)
            high_ref[t * ORB:(t + 1) * ORB, along] = high
            low_ref[t * ORB:(t + 1) * ORB, along] = low

    build_triangle(big, big_hi, big_lo, CHIP)
    for ref in (big_hi, big_lo):
        for a in range(3):
            tile = slice(a * TILE, (a + 1) * TILE)
            ref[tile, tile] = symmetrized(ref[tile, tile])
    for s in range(ROWS):
        forward(s, 0).wait_recv()
    build_triangle(small, small_hi, small_lo, ROWS)
    for ref in (small_hi, small_lo):
        ref[...] = symmetrized(ref[...])

    corners(left, square)
    for along in (slice(0, SIDE), slice(2 * SIDE, FRAME)):
        masked = square[:, along] * maskrow[0:1, along]
        square[:, along] = masked
        stack(middle, masked, along)
    sides(middle, cube)
    corners(middle, cube)

    result = 3.0 * square[...] - 2.0 * (cube[...] * maskrow[0:1, :])
    out[0] = pltpu.roll(result, FRAME - place * ORB, 1)[:, 0:BAND]

    drain()


def on_device(density, pattern):
    dma = pltpu.SemaphoreType.DMA
    return pl.pallas_call(
        kernel,
        out_shape=jax.ShapeDtypeStruct((1, ORB, BAND), F32),
        in_specs=[pl.BlockSpec(memory_space=pltpu.HBM)] * 2,
        out_specs=pl.BlockSpec(memory_space=pltpu.VMEM),
        scratch_shapes=[
            pltpu.SMEM((ROWS, 25), jnp.int32),
            pltpu.VMEM((CHIP, ORB, BAND), F32),
            pltpu.VMEM((CHIP, ORB, SIDE), F32),
            pltpu.VMEM((ROWS, ORB, HALFSIDE), F32),
            pltpu.VMEM((SIDE, FRAME), BF16),
            pltpu.VMEM((SIDE, FRAME), BF16),
            pltpu.VMEM((SIDE, SIDE), BF16),
            pltpu.VMEM((SIDE, SIDE), BF16),
            pltpu.VMEM((HALFSIDE, HALFSIDE), BF16),
            pltpu.VMEM((HALFSIDE, HALFSIDE), BF16),
            pltpu.VMEM((2 * ORB, FRAME), BF16),
            pltpu.VMEM((2 * ORB, FRAME), BF16),
            pltpu.VMEM((ORB, FRAME), F32),
            pltpu.VMEM((ORB, FRAME), F32),
            pltpu.VMEM((8, FRAME), F32),
            dma, dma, dma, dma, dma((CHIP,)), dma((CHIP,)), dma((PIECES,)), dma((ROWS,)), dma((ROWS,)),
            dma((5, PIECES)), pltpu.SemaphoreType.REGULAR((SLOTS + 4,)),
        ],
        compiler_params=pltpu.CompilerParams(
            collective_id=0, has_side_effects=True, vmem_limit_bytes=VMEM_LIMIT
        ),
    )(density, pattern)


def solution(mesh):
    in_specs = (P("wire", None, None), P("wire", None))
    out_specs = P(("wire", "depth"), None, None)
    return jax.shard_map(
        on_device, mesh=mesh, in_specs=in_specs, out_specs=out_specs, check_vma=False
    )
```
